256 devices in a mesh: block: 8 (over x_lo, y), tile: 32 (over z, x_hi, core).
Axes of the slice: x: 4 (x_hi: 2, x_lo: 2; x = x_hi * 2 + x_lo), y: 4, z: 8, core: 2. Of those that a mesh axis runs over, the one named last changes fastest.
Arguments:
- inputs: bfloat16 [32, 64, 96, 256], P('block', 'tile'), may hold values from -600 to 600
- out_grads: bfloat16 [32, 64, 96, 256], P('block', 'tile'), may hold values from -150 to 150
- kernel: bfloat16 [3, 3, 96, 3, 96], replicated, may hold values from -0.125 to 0.125
- norm_gain: float32 [96], replicated, may hold values from 0.1 to 1.9
- norm_shift: float32 [96], replicated, may hold values from -3 to 3
Outputs:
- input_grad: bfloat16 [32, 64, 96, 256], P('block', 'tile')
- kernel_grad: float32 [3, 3, 96, 3, 96], replicated
- gain_grad: float32 [96], replicated
- shift_grad: float32 [96], replicated
The draws below stay inside these ranges and needn't reach their ends.
All inputs are finite; a program needn't handle non-finite values.
Results may differ from the reference program's by a relative error of at most 0.006.
Values may be sent and summed in bfloat16 or wider, within the bound.
A program may use at most 64 MiB of HBM per device.

```python
import math
import jax
import jax.numpy as jnp
from jax import lax

C = 96
GROUPS = 32
WID = 256
HEIGHT = 64
ALL_FRAMES = 32


def field_scales(key):
    row_key, col_key = jax.random.split(key)
    rising = 3.0 ** (jnp.arange(HEIGHT, dtype=jnp.float32) / HEIGHT)
    row_scale = rising * jnp.exp(jax.random.uniform(row_key, (HEIGHT,), jnp.float32, 0.0, math.log(3.3)))
    col_scale = jnp.exp(jax.random.uniform(col_key, (WID,), jnp.float32, 0.0, math.log(10.0)))
    return row_scale[None, :, None, None] * col_scale[None, None, None, :]


def draw_inputs(key, part):
    key = jax.random.fold_in(key, 7)
    base_key, scale_key = jax.random.split(key)
    shape = (ALL_FRAMES, HEIGHT, C, WID)
    base = jnp.clip(jax.random.normal(base_key, shape, jnp.float32), -6.0, 6.0)
    return (base * field_scales(scale_key)).astype(jnp.bfloat16)


def draw_out_grads(key, part):
    key = jax.random.fold_in(key, 13)
    base_key, scale_key = jax.random.split(key)
    shape = (ALL_FRAMES, HEIGHT, C, WID)
    base = jnp.clip(jax.random.normal(base_key, shape, jnp.float32), -6.0, 6.0)
    return (0.25 * base * field_scales(scale_key)).astype(jnp.bfloat16)


def scatter_about(rng, shape, deviation, reach, kind=jnp.bfloat16):
    values = deviation * jax.random.normal(rng, shape, jnp.float32)
    return jnp.clip(values, min=-reach, max=reach).astype(kind)


def setup_inputs(seed: int = 0) -> dict:
    key_list = jax.random.split(jax.random.key(seed), 6)
    inputs = draw_inputs(jax.random.fold_in(key_list[5], 71), 0)
    out_grads = draw_out_grads(jax.random.fold_in(key_list[5], 71), 0)
    kernel = scatter_about(key_list[2], (3, 3, C, 3, C), (27 * C) ** -0.5, 0.125)
    norm_gain = jnp.clip(1.0 + 0.18 * jax.random.normal(key_list[3], (C,), jnp.float32), 0.1, 1.9)
    norm_shift = scatter_about(key_list[4], (C,), 0.5, 3.0, jnp.float32)
    return dict(inputs=inputs, out_grads=out_grads, kernel=kernel, norm_gain=norm_gain, norm_shift=norm_shift)


loss_scale = 1024.0
epsilon = 1e-06

def activate(frame, norm_gain, norm_shift):
    row_count, channels, columns = frame.shape
    grouped = frame.astype(jnp.float32).reshape(row_count, GROUPS, channels // GROUPS, columns)
    center = lax.optimization_barrier(jnp.mean(grouped, axis=(0, 2, 3)))
    spread = lax.rsqrt(lax.optimization_barrier(jnp.mean(grouped * grouped, axis=(0, 2, 3))) - center * center + epsilon)
    normed = ((grouped - center[None, :, None, None]) * spread[None, :, None, None]).reshape(row_count, channels, columns)
    shaped = normed * norm_gain[None, :, None] + norm_shift[None, :, None]
    return (normed, shaped, spread)

def reference(inputs, out_grads, kernel, norm_gain, norm_shift):

    def frame_acts(frame):
        return jax.nn.silu(activate(frame, norm_gain, norm_shift)[1]).astype(jnp.bfloat16)
    acts = lax.map(frame_acts, inputs)
    act_pad = jnp.pad(acts, ((2, 0), (1, 1), (0, 0), (1, 1)))
    grad_pad = jnp.pad(out_grads, ((0, 2), (1, 1), (0, 0), (1, 1)))
    indices = jnp.arange(ALL_FRAMES, dtype=jnp.int32)

    def kernel_step(carry, index):
        window = lax.dynamic_slice_in_dim(act_pad, index, 3, 0).astype(jnp.float32)
        current = lax.dynamic_index_in_dim(out_grads, index, 0, keepdims=False).astype(jnp.float32)
        partials = []
        for time_tap in range(3):
            for row_tap in range(3):
                stacked = jnp.concatenate([window[time_tap, row_tap:row_tap + HEIGHT, :, col_tap:col_tap + WID] for col_tap in range(3)], axis=1)
                partials.append(jnp.einsum('how,hkw->ok', current, stacked))
        return (carry + jnp.stack(partials).reshape(3, 3, C, 3, C), None)
    weight_sum, _ = lax.scan(kernel_step, jnp.zeros((3, 3, C, 3, C), jnp.float32), indices)

    def frame_grad(index):
        window = lax.dynamic_slice_in_dim(grad_pad, index, 3, 0).astype(jnp.float32)
        summed = jnp.zeros((HEIGHT, C, WID), jnp.float32)
        for time_tap in range(3):
            for row_tap in range(3):
                stacked = jnp.concatenate([window[2 - time_tap, 2 - row_tap:2 - row_tap + HEIGHT, :, 2 - col_tap:2 - col_tap + WID] for col_tap in range(3)], axis=1)
                weights = kernel[time_tap, row_tap].astype(jnp.float32).transpose(1, 0, 2).reshape(3 * C, C)
                summed = summed + jnp.einsum('hkw,ki->hiw', stacked, weights)
        frame = lax.dynamic_index_in_dim(inputs, index, 0, keepdims=False)
        normed, shaped, spread = activate(frame, norm_gain, norm_shift)
        logistic = jax.nn.sigmoid(shaped)
        pre_grad = summed * logistic * (1.0 + shaped * (1.0 - logistic))
        norm_grad = pre_grad * norm_gain[None, :, None]
        grouped_grad = norm_grad.reshape(HEIGHT, GROUPS, C // GROUPS, WID)
        grouped_norm = normed.reshape(HEIGHT, GROUPS, C // GROUPS, WID)
        first_mean = lax.optimization_barrier(jnp.mean(grouped_grad, axis=(0, 2, 3)))
        second_mean = lax.optimization_barrier(jnp.mean(grouped_grad * grouped_norm, axis=(0, 2, 3)))
        result = spread[None, :, None, None] * (grouped_grad - first_mean[None, :, None, None] - grouped_norm * second_mean[None, :, None, None])
        return (result.reshape(HEIGHT, C, WID).astype(jnp.bfloat16), lax.optimization_barrier(jnp.sum(pre_grad * normed, axis=(0, 2))), lax.optimization_barrier(jnp.sum(pre_grad, axis=(0, 2))))
    input_grad, gain_terms, shift_terms = lax.map(frame_grad, indices)
    return (input_grad, weight_sum / loss_scale, lax.optimization_barrier(jnp.sum(gain_terms, axis=0)) / loss_scale, lax.optimization_barrier(jnp.sum(shift_terms, axis=0)) / loss_scale)
```

```python
import functools

import jax
import jax.numpy as jnp
from jax import lax
from jax.experimental import pallas as pl
from jax.experimental.pallas import tpu as pltpu
from jax.sharding import PartitionSpec as P

MESH = pl.DeviceIdType.MESH
GROUPS = 32
LOSS_SCALE = 1024.0
EPSILON = 1e-06
F32 = jnp.float32
BF16 = jnp.bfloat16

FRAMES, ROWS, CH, COLS = 4, 2, 96, 256
TAPS = 9 * CH
KEPT = TAPS // 4
SPLIT = TAPS - KEPT
FLAT = 2048
HALF = FLAT // 2


def group_sum(values, lane):
    place = lax.rem(lane, 3)
    one_up = pltpu.roll(values, 127, 1)
    two_up = pltpu.roll(values, 126, 1)
    one_down = pltpu.roll(values, 1, 1)
    two_down = pltpu.roll(values, 2, 1)
    first = jnp.where(place == 0, one_up, one_down)
    second = jnp.where(place == 2, two_down, jnp.where(place == 0, two_up, one_up))
    return values + first + second


def body(
    sizes,
    x_hbm, g_hbm, w_hbm, gain_ref, shift_ref,
    out_hbm, kg_hbm, small_ref,
    xv, gp, wv, wst, factor, normed, acts, acc, pre, outv,
    packed, core_send, core_got, plane_send, plane_got, z_send, z_got, fin_send, fin_got,
    final, plane_fin, kg_out, tmat, st_send, quad_got, st_mid, col_got, blk_send, blk_got,
    loc_sem, ssem, rsem,
):
    nb, nz = sizes
    ny = nb // 2
    plane = 2 * nb
    share = HALF // plane
    zshare = share // nz
    b = lax.axis_index("block")
    t = lax.axis_index("tile")
    nt = 4 * nz
    z = t // 4
    xh = lax.rem(t, 4) // 2
    c = lax.rem(t, 2)
    xl, y = b // ny, lax.rem(b, ny)
    flip_c = t + 1 - 2 * c
    flip_x = t + 2 - 4 * xh
    flip_cx = flip_c + 2 - 4 * xh
    across = lax.rem(t + nt - 1 + 2 * c, nt)
    b_up = lax.rem(b + 1, nb)
    b_down = lax.rem(b + nb - 1, nb)
    me = xh * nb + b

    counter = [0]

    def remote(src, dst, device):
        i = counter[0]
        counter[0] += 1
        return pltpu.make_async_remote_copy(
            src_ref=src, dst_ref=dst, send_sem=ssem.at[i], recv_sem=rsem.at[i],
            device_id=device, device_id_type=MESH,
        )

    def plane_at(dx, dy):
        x = lax.rem(2 * xh + xl + dx, 4)
        yy = lax.rem(y + dy, ny)
        hi, lo = x // 2, lax.rem(x, 2)
        block = lo * ny + yy
        return hi * nb + block, (block, t + 2 * (hi - xh))

    steps = [(dx, dy) for dx in range(4) for dy in range(ny) if (dx, dy) != (0, 0)]
    to_plane = [plane_at(dx, dy) for dx, dy in steps]
    from_plane = [plane_at((4 - dx) % 4, (ny - dy) % ny) for dx, dy in steps]

    load_x = pltpu.make_async_copy(x_hbm, xv, loc_sem.at[0])
    load_g = pltpu.make_async_copy(g_hbm, gp.at[pl.ds(0, FRAMES), pl.ds(1, ROWS)], loc_sem.at[1])
    load_w = pltpu.make_async_copy(w_hbm, wv, loc_sem.at[2])
    load_x.start()
    load_g.start()
    load_w.start()

    barrier = pltpu.get_barrier_semaphore()
    friends = [device for _, device in to_plane]
    for d in range(1, nz):
        friends.append((b, lax.rem(t + 4 * d, nt)))
    for tile in (flip_c, across):
        for block in (b, b_up, b_down):
            friends.append((block, tile))
    friends.append((b, flip_cx))
    for device in friends:
        pl.semaphore_signal(barrier, inc=1, device_id=device, device_id_type=MESH)

    lane = lax.broadcasted_iota(jnp.int32, (CH, 128), 1)
    lane8 = lax.broadcasted_iota(jnp.int32, (8, 128), 1)
    row8 = lax.broadcasted_iota(jnp.int32, (8, 128), 0)
    col = lax.broadcasted_iota(jnp.int32, (CH, COLS), 1)
    tmat[...] = jnp.zeros((128, 128), F32)

    def channel_tile(columns):
        table = jnp.zeros((CH, 128), F32)
        for k, value in enumerate(columns):
            table = jnp.where(lane == k, value, table)
        tmat[0:CH, :] = table
        return tmat[...].T[0:8, :]

    def channel_columns(tile):
        tmat[0:8, :] = tile
        return tmat[...].T[0:CH, :]

    def halved(value):
        return value[:, 0:128] + value[:, 128:256]

    load_x.wait()
    firsts, seconds = [], []
    for f in range(FRAMES):
        one, two = jnp.zeros((CH, 128), F32), jnp.zeros((CH, 128), F32)
        for r in range(ROWS):
            value = xv[f, r].astype(F32)
            one = one + halved(value)
            two = two + halved(value * value)
        firsts.append(jnp.sum(one, axis=1, keepdims=True))
        seconds.append(jnp.sum(two, axis=1, keepdims=True))
    st_send[0] = channel_tile(firsts + seconds)

    pl.semaphore_wait(barrier, len(friends))

    inner_low, inner_high = t > 0, t < nt - 1
    has_down, has_up = b > 0, b < nb - 1
    t_low, t_high = lax.rem(t + nt - 1, nt), lax.rem(t + 1, nt)
    four, two = pl.ds(0, FRAMES), pl.ds(0, 2)
    late = pl.ds(FRAMES, 2)
    halos = []
    for src, dst, device, sends, gets in (
        (g_hbm.at[four, 1], gp.at[four, 0], (b, t_high), inner_high, inner_low),
        (g_hbm.at[four, 0], gp.at[four, 3], (b, t_low), inner_low, inner_high),
        (g_hbm.at[two], gp.at[late, pl.ds(1, ROWS)], (b_down, t), has_down, has_up),
        (g_hbm.at[two, 1], gp.at[late, 0], (b_down, t_high),
         jnp.logical_and(has_down, inner_high), jnp.logical_and(has_up, inner_low)),
        (g_hbm.at[two, 0], gp.at[late, 3], (b_down, t_low),
         jnp.logical_and(has_down, inner_low), jnp.logical_and(has_up, inner_high)),
    ):
        halos.append((remote(src, dst, device), sends, gets))

    def all_sum(tile, at):
        quad = 2 * xh + c
        copies = []
        for k, other in enumerate((flip_c, flip_x, flip_cx)):
            slot = lax.rem(other, 4)
            copies.append((
                remote(st_send.at[at], quad_got.at[at, quad], (b, other)),
                quad_got.at[at, slot],
            ))
        for copy, _ in copies:
            copy.start()
        quad_got[at, quad] = tile
        return copies

    def quad_sum(copies, at):
        for copy, _ in copies:
            copy.wait_recv()
        total = quad_got[at, 0]
        for k in range(1, 4):
            total = total + quad_got[at, k]
        st_mid[at] = total
        out = []
        for d in range(1, nz):
            out.append(remote(st_mid.at[at], col_got.at[at, z], (b, lax.rem(t + 4 * d, nt))))
        for copy in out:
            copy.start()
        col_got[at, z] = total
        return out

    def col_sum(copies, at):
        for copy in copies:
            copy.wait_recv()
        total = col_got[at, 0]
        for k in range(1, nz):
            total = total + col_got[at, k]
        return total

    waiting = []
    stat_copies = all_sum(st_send[0], 0)
    for copy, sends, _ in halos:
        pl.when(sends)(copy.start)

    @pl.when(jnp.logical_not(inner_low))
    def _():
        gp[:, 0] = jnp.zeros((FRAMES + 2, CH, COLS), BF16)

    @pl.when(jnp.logical_not(inner_high))
    def _():
        gp[:, 3] = jnp.zeros((FRAMES + 2, CH, COLS), BF16)

    @pl.when(jnp.logical_not(has_up))
    def _():
        gp[late] = jnp.zeros((2, 4, CH, COLS), BF16)

    stat_copies_z = quad_sum(stat_copies, 0)
    waiting += [copy for copy, _ in stat_copies] + stat_copies_z

    load_w.wait()
    for r in range(3):
        slab = jnp.concatenate(
            [wv[2 - p, 2 - q, r] for p in range(3) for q in range(3)], axis=0
        )
        wst[r * CH : (r + 1) * CH, :] = slab.astype(F32).T.astype(BF16)

    number = float(nt * ROWS * COLS * (CH // GROUPS))
    sums = group_sum(col_sum(stat_copies_z, 0), lane8) / number
    center_rows = sums
    square_rows = pltpu.roll(sums, 4, 0)
    spread_rows = lax.rsqrt(square_rows - center_rows * center_rows + EPSILON)
    both = jnp.where(row8 < 4, center_rows, pltpu.roll(spread_rows, 4, 0))
    stats = channel_columns(both)
    vectors = jnp.where(
        row8 == 0,
        jnp.broadcast_to(gain_ref[...], (8, 128)),
        jnp.broadcast_to(shift_ref[...], (8, 128)),
    )
    vectors = channel_columns(vectors)
    gain, shift = vectors[:, 0:1], vectors[:, 1:2]

    acts[...] = jnp.zeros_like(acts)
    for f in range(FRAMES):
        center, spread = stats[:, f : f + 1], stats[:, 4 + f : 5 + f]
        for r in range(ROWS):
            n = f * ROWS + r
            scaled = (xv[f, r].astype(F32) - center) * spread
            shaped = scaled * gain + shift
            logistic = 1.0 / (1.0 + jnp.exp(-shaped))
            active = shaped * logistic
            normed[n] = scaled
            factor[n] = logistic * (1.0 + shaped * (1.0 - logistic))
            before = jnp.where(col == 0, 0.0, pltpu.roll(active, 1, 1))
            after = jnp.where(col == COLS - 1, 0.0, pltpu.roll(active, COLS - 1, 1))
            acts[n, 0:CH] = before.astype(BF16)
            acts[n, 128 : 128 + CH] = active.astype(BF16)
            acts[n, 256 : 256 + CH] = after.astype(BF16)

    load_g.wait()
    for copy, _, gets in halos:
        pl.when(gets)(copy.wait_recv)

    def kernel_term(n):
        f, r = n // ROWS, lax.rem(n, ROWS)
        window = gp[pl.ds(f, 3), pl.ds(r, 3)].reshape(TAPS, COLS)
        return lax.dot_general(
            window, acts[n], (((1,), (1,)), ((), ())), preferred_element_type=F32
        )

    acc[...] = kernel_term(0)

    @pl.loop(1, FRAMES * ROWS)
    def _(n):
        acc[...] += kernel_term(n)

    lanes = lax.broadcasted_iota(jnp.int32, (KEPT, 128), 1)
    for k in range(3):
        for s in range(3):
            row = KEPT * (3 * k + s)
            slab, first = row // TAPS, row % TAPS
            extra = acc[KEPT * (s + 1) : KEPT * (s + 2), 256:384]
            extra = pltpu.roll(extra, CH - 32 * k, 1)
            packed[row : row + KEPT] = jnp.where(
                lanes < CH, acc[first : first + KEPT, 128 * slab : 128 * slab + 128], extra
            )
    packed[9 * KEPT : FLAT] = jnp.zeros((FLAT - 9 * KEPT, 128), F32)

    mine = pl.multiple_of(c * HALF, HALF)
    theirs = pl.multiple_of((1 - c) * HALF, HALF)
    core_send[...] = packed[pl.ds(theirs, HALF)].astype(BF16)
    core_copy = remote(core_send, core_got, (b, flip_c))
    core_copy.start()

    @pl.loop(0, FRAMES * ROWS)
    def _(n):
        f, r = n // ROWS, lax.rem(n, ROWS)
        window = gp[pl.ds(f, 3), pl.ds(r, 3)].reshape(TAPS, COLS)
        product = jnp.dot(wst[...], window, preferred_element_type=F32)
        after = pltpu.roll(product[0:CH], COLS - 1, 1)
        before = pltpu.roll(product[2 * CH : 3 * CH], 1, 1)
        after = jnp.where(col == COLS - 1, 0.0, after)
        before = jnp.where(col == 0, 0.0, before)
        pre[n] = (after + product[CH : 2 * CH] + before) * factor[n]

    core_copy.wait_recv()
    chip = packed[pl.ds(mine, HALF)] + core_got[...].astype(F32)
    packed[pl.ds(mine, HALF)] = chip
    plane_send[...] = chip.astype(BF16)
    plane_copies = []
    for k, (place, device) in enumerate(to_plane):
        rows = pl.ds(pl.multiple_of(place * share, share), share)
        plane_copies.append(remote(plane_send.at[rows], plane_got.at[k], device))
    for copy in plane_copies:
        copy.start()

    firsts, seconds = [], []
    for f in range(FRAMES):
        one, two = jnp.zeros((CH, 128), F32), jnp.zeros((CH, 128), F32)
        for r in range(ROWS):
            n = f * ROWS + r
            value = pre[n]
            one = one + halved(value)
            two = two + halved(value * normed[n])
        firsts.append(jnp.sum(one, axis=1, keepdims=True))
        seconds.append(jnp.sum(two, axis=1, keepdims=True))
    tmat[...] = jnp.zeros((128, 128), F32)
    st_send[1] = channel_tile(firsts + seconds)
    stat_copies = all_sum(st_send[1], 1)

    for copy in plane_copies:
        copy.wait_recv()
    part = packed[pl.ds(pl.multiple_of(mine + me * share, share), share)]
    for k in range(plane - 1):
        part = part + plane_got[k].astype(F32)
    z_send[...] = part
    z_copies = []
    for d in range(1, nz):
        there = lax.rem(z + d, nz)
        rows = pl.ds(pl.multiple_of(there * zshare, zshare), zshare)
        z_copies.append(remote(z_send.at[rows], z_got.at[d], (b, lax.rem(t + 4 * d, nt))))
    for copy in z_copies:
        copy.start()

    stat_copies_z = quad_sum(stat_copies, 1)
    waiting += [copy for copy, _ in stat_copies] + stat_copies_z

    for copy in z_copies:
        copy.wait_recv()
    here = pl.ds(pl.multiple_of(z * zshare, zshare), zshare)
    part = z_send[here]
    for d in range(1, nz):
        part = part + z_got[d]
    fin_send[...] = part
    fin_got[here] = part
    fin_copies = []
    for d in range(1, nz):
        fin_copies.append(remote(fin_send, fin_got.at[here], (b, lax.rem(t + 4 * d, nt))))
    for copy in fin_copies:
        copy.start()

    total = col_sum(stat_copies_z, 1)
    gain_rows = jnp.broadcast_to(gain_ref[...], (8, 128))
    means = channel_columns(group_sum(total * gain_rows, lane8) / number)

    pairs = total + pltpu.roll(total, 2, 0)
    pairs = pairs + pltpu.roll(pairs, 1, 0)
    blk_send[...] = pairs
    blk_got[b] = pairs
    blk_copies = []
    for d in range(1, nb):
        block = lax.rem(b + d, nb)
        blk_copies.append(remote(blk_send, blk_got.at[b], (block, t)))
    for copy in blk_copies:
        copy.start()

    for copy in fin_copies:
        copy.wait_recv()
    plane_fin[...] = fin_got[...].astype(BF16)
    own_rows = pl.ds(pl.multiple_of(mine + me * share, share), share)
    final[own_rows] = plane_fin[...]
    spread_copies = []
    for place, device in to_plane:
        spread_copies.append(remote(plane_fin, final.at[own_rows], device))
    for copy in spread_copies:
        copy.start()
    pass_copies = [remote(plane_fin, final.at[own_rows], (b, flip_c))]
    pass_copies[0].start()

    for f in range(FRAMES):
        spread = stats[:, 4 + f : 5 + f]
        m1, m2 = means[:, f : f + 1], means[:, 4 + f : 5 + f]
        for r in range(ROWS):
            n = f * ROWS + r
            value = spread * (pre[n] * gain - m1 - normed[n] * m2)
            outv[f, r] = value.astype(BF16)
    store_x = pltpu.make_async_copy(outv, out_hbm, loc_sem.at[3])
    store_x.start()

    for copy in blk_copies:
        copy.wait_recv()
    total = blk_got[0]
    for k in range(1, nb):
        total = total + blk_got[k]
    small_ref[...] = total / LOSS_SCALE

    for copy, (place, _) in zip(spread_copies, from_plane):
        copy.wait_recv()
        rows = pl.ds(pl.multiple_of(mine + place * share, share), share)
        pass_copies.append(remote(final.at[rows], final.at[rows], (b, flip_c)))
        pass_copies[-1].start()
    for copy in pass_copies:
        copy.wait_recv()

    packed[...] = final[...].astype(F32) * (1.0 / LOSS_SCALE)
    for p in range(3):
        for q in range(3):
            tap = (2 - p) * 3 + (2 - q)
            for r in range(2):
                row = r * TAPS + tap * CH
                kg_out[p, q, r] = packed[row : row + CH, 0:CH]
    for tap in range(9):
        p, q = 2 - tap // 3, 2 - tap % 3
        for first in range(tap * CH, tap * CH + CH, 8):
            local = first - tap * CH
            if first < KEPT:
                slab = packed[2 * TAPS + first : 2 * TAPS + first + 8]
            else:
                slab = jnp.zeros((8, 128), F32)
                for k in range(3):
                    row = 3 * KEPT * k + first - KEPT
                    piece = pltpu.roll(packed[row : row + 8], 32 + 32 * k, 1)
                    slab = jnp.where(lane8 // 32 == k, piece, slab)
            kg_out[p, q, 2, local : local + 8] = slab[:, 0:CH]
    store_k = pltpu.make_async_copy(kg_out, kg_hbm, loc_sem.at[4])
    store_k.start()

    for copy, sends, _ in halos:
        pl.when(sends)(copy.wait_send)
    waiting += [core_copy] + plane_copies + z_copies + fin_copies + blk_copies
    waiting += spread_copies + pass_copies
    for copy in waiting:
        copy.wait_send()
    store_x.wait()
    store_k.wait()


def shards(sizes, inputs, out_grads, kernel, norm_gain, norm_shift):
    nb, nz = sizes
    plane = 2 * nb
    share = HALF // plane
    copies = 5 + 2 * (3 + nz - 1) + 1 + 2 * (plane - 1) + 2 * (nz - 1) + nb - 1 + plane
    vmem = pltpu.VMEM
    pad = lambda v: jnp.pad(v, (0, 128 - CH)).reshape(1, 128)
    any_space = pl.BlockSpec(memory_space=pl.ANY)
    in_vmem = pl.BlockSpec(memory_space=pltpu.VMEM)
    cells = FRAMES * ROWS
    out, grad, small = pl.pallas_call(
        functools.partial(body, sizes),
        out_shape=(
            jax.ShapeDtypeStruct((FRAMES, ROWS, CH, COLS), BF16),
            jax.ShapeDtypeStruct((3, 3, 3, CH, CH), F32),
            jax.ShapeDtypeStruct((8, 128), F32),
        ),
        in_specs=[any_space] * 3 + [in_vmem] * 2,
        out_specs=(any_space, any_space, in_vmem),
        scratch_shapes=[
            vmem((FRAMES, ROWS, CH, COLS), BF16),
            vmem((FRAMES + 2, ROWS + 2, CH, COLS), BF16),
            vmem((3, 3, 3, CH, CH), BF16),
            vmem((3 * CH, TAPS), BF16),
            vmem((cells, CH, COLS), F32),
            vmem((cells, CH, COLS), F32),
            vmem((cells, 3 * 128, COLS), BF16),
            vmem((TAPS, 3 * 128), F32),
            vmem((cells, CH, COLS), F32),
            vmem((FRAMES, ROWS, CH, COLS), BF16),
            vmem((FLAT, 128), F32),
            vmem((HALF, 128), BF16),
            vmem((HALF, 128), BF16),
            vmem((HALF, 128), BF16),
            vmem((plane - 1, share, 128), BF16),
            vmem((share, 128), F32),
            vmem((nz, share // nz, 128), F32),
            vmem((share // nz, 128), F32),
            vmem((share, 128), F32),
            vmem((FLAT, 128), BF16),
            vmem((share, 128), BF16),
            vmem((3, 3, 3, CH, CH), F32),
            vmem((128, 128), F32),
            vmem((2, 8, 128), F32),
            vmem((2, 4, 8, 128), F32),
            vmem((2, 8, 128), F32),
            vmem((2, nz, 8, 128), F32),
            vmem((8, 128), F32),
            vmem((nb, 8, 128), F32),
            pltpu.SemaphoreType.DMA((5,)),
            pltpu.SemaphoreType.DMA((copies,)),
            pltpu.SemaphoreType.DMA((copies,)),
        ],
        compiler_params=pltpu.CompilerParams(
            collective_id=0, has_side_effects=True, vmem_limit_bytes=40 * 1024 * 1024
        ),
    )(inputs, out_grads, kernel.transpose(0, 1, 3, 2, 4), pad(norm_gain), pad(norm_shift))
    return (out, grad.transpose(0, 1, 3, 2, 4), small[7, :CH], small[3, :CH])


def solution(mesh):
    sizes = (mesh.shape["block"], mesh.shape["tile"] // 4)
    placed = (P("block", "tile", None, None), P("block", "tile", None, None), P(), P(), P())
    return jax.shard_map(
        functools.partial(shards, sizes),
        mesh=mesh,
        in_specs=placed,
        out_specs=(P("block", "tile", None, None), P(), P(), P()),
        check_vma=False,
    )
```

```python
import functools

import jax
import jax.numpy as jnp
from jax import lax
from jax.experimental import pallas as pl
from jax.experimental.pallas import tpu as pltpu
from jax.sharding import PartitionSpec as P

MESH = pl.DeviceIdType.MESH
GROUPS = 32
LOSS_SCALE = 1024.0
EPSILON = 1e-06
F32 = jnp.float32
BF16 = jnp.bfloat16

FRAMES, ROWS, CH, COLS = 4, 2, 96, 256
TAPS = 9 * CH
KEPT = 240
MOVED = TAPS - KEPT
SEG = 48
FLAT = 2048
HALF = FLAT // 2


def group_sum(values, lane):
    place = lax.rem(lane, 3)
    one_up = pltpu.roll(values, 127, 1)
    two_up = pltpu.roll(values, 126, 1)
    one_down = pltpu.roll(values, 1, 1)
    two_down = pltpu.roll(values, 2, 1)
    first = jnp.where(place == 0, one_up, one_down)
    second = jnp.where(place == 2, two_down, jnp.where(place == 0, two_up, one_up))
    return values + first + second


def body(
    sizes,
    x_hbm, g_hbm, w_hbm, gain_hbm, shift_hbm,
    out_hbm, fin_hbm, small_hbm,
    gain_ref, shift_ref, outv, small_ref, xv, gp, wv, wst, factor, normed, acts, acc, pre,
    packed, core_send, core_got, plane_send, plane_got, z_send, z_got,
    final, plane_fin, tmat, st_send, quad_got, st_mid, col_got, blk_send, blk_got,
    loc_sem, ssem, rsem,
):
    nb, nz = sizes
    ny = nb // 2
    plane = 2 * nb
    share = HALF // plane
    b = lax.axis_index("block")
    t = lax.axis_index("tile")
    nt = 4 * nz
    z = t // 4
    xh = lax.rem(t, 4) // 2
    c = lax.rem(t, 2)
    xl, y = b // ny, lax.rem(b, ny)
    flip_c = t + 1 - 2 * c
    flip_x = t + 2 - 4 * xh
    flip_cx = flip_c + 2 - 4 * xh
    across = lax.rem(t + nt - 1 + 2 * c, nt)
    b_up = lax.rem(b + 1, nb)
    b_down = lax.rem(b + nb - 1, nb)
    me = xh * nb + b

    counter = [0]

    def remote(src, dst, device):
        i = counter[0]
        counter[0] += 1
        return pltpu.make_async_remote_copy(
            src_ref=src, dst_ref=dst, send_sem=ssem.at[i], recv_sem=rsem.at[i],
            device_id=device, device_id_type=MESH,
        )

    def plane_at(dx, dy):
        x = lax.rem(2 * xh + xl + dx, 4)
        yy = lax.rem(y + dy, ny)
        hi, lo = x // 2, lax.rem(x, 2)
        block = lo * ny + yy
        return hi * nb + block, (block, t + 2 * (hi - xh))

    steps = [(dx, dy) for dx in range(4) for dy in range(ny) if (dx, dy) != (0, 0)]
    steps.sort(key=lambda d: -min(d[0], 4 - d[0]) - min(d[1], ny - d[1]))
    to_plane = [plane_at(dx, dy) for dx, dy in steps]
    from_plane = [plane_at((4 - dx) % 4, (ny - dy) % ny) for dx, dy in steps]

    load_x = pltpu.make_async_copy(x_hbm, xv, loc_sem.at[0])
    load_g = pltpu.make_async_copy(g_hbm, gp.at[pl.ds(0, FRAMES), pl.ds(1, ROWS)], loc_sem.at[1])
    load_w = pltpu.make_async_copy(w_hbm, wv, loc_sem.at[2])
    load_gain = pltpu.make_async_copy(gain_hbm, gain_ref, loc_sem.at[3])
    load_shift = pltpu.make_async_copy(shift_hbm, shift_ref, loc_sem.at[4])
    load_x.start()
    load_g.start()
    load_gain.start()
    load_shift.start()
    load_w.start()

    barrier = pltpu.get_barrier_semaphore()
    friends = [device for _, device in to_plane]
    far_first = sorted(range(1, nz), key=lambda d: -min(d, nz - d))
    column = [(b, lax.rem(t + 4 * d, nt)) for d in far_first]
    friends += column
    friends += [(b, across), (b_up, across), (b_down, across), (b, flip_c), (b, flip_cx)]
    for device in friends:
        pl.semaphore_signal(barrier, inc=1, device_id=device, device_id_type=MESH)

    lane = lax.broadcasted_iota(jnp.int32, (CH, 128), 1)
    lane8 = lax.broadcasted_iota(jnp.int32, (8, 128), 1)
    row8 = lax.broadcasted_iota(jnp.int32, (8, 128), 0)
    col = lax.broadcasted_iota(jnp.int32, (CH, COLS), 1)
    tmat[...] = jnp.zeros((128, 128), F32)

    def channel_tile(columns):
        table = jnp.zeros((CH, 128), F32)
        for k, value in enumerate(columns):
            table = jnp.where(lane == k, value, table)
        tmat[0:CH, :] = table
        return tmat[...].T[0:8, :]

    def channel_columns(tile):
        tmat[0:8, :] = tile
        return tmat[...].T[0:CH, :]

    def halved(value):
        return value[:, 0:128] + value[:, 128:256]

    load_x.wait()
    firsts, seconds = [], []
    for f in range(FRAMES):
        one, two = jnp.zeros((CH, 128), F32), jnp.zeros((CH, 128), F32)
        for r in range(ROWS):
            value = xv[f, r].astype(F32)
            one = one + halved(value)
            two = two + halved(value * value)
        firsts.append(jnp.sum(one, axis=1, keepdims=True))
        seconds.append(jnp.sum(two, axis=1, keepdims=True))
    st_send[0] = channel_tile(firsts + seconds)

    pl.semaphore_wait(barrier, len(friends))

    has_across = jnp.where(c == 0, t > 0, t < nt - 1)
    has_down, has_up = b > 0, b < nb - 1
    four, two, late = pl.ds(0, FRAMES), pl.ds(0, 2), pl.ds(FRAMES, 2)
    core_edge, far_edge = 3 - 3 * c, 3 * c
    rows_far = remote(g_hbm.at[four, c], gp.at[four, 3 - 3 * c], (b, across))
    rows_core = remote(g_hbm.at[four, 1 - c], gp.at[four, 3 * c], (b, flip_c))
    next_two = remote(g_hbm.at[two], gp.at[late, pl.ds(1, ROWS)], (b_down, t))
    corner_far = remote(g_hbm.at[two, c], gp.at[late, 3 - 3 * c], (b_down, across))
    corner_core = remote(gp.at[late, 2 - c], gp.at[late, 3 * c], (b, flip_c))

    def all_sum(tile, at):
        quad = 2 * xh + c
        copies = []
        for k, other in enumerate((flip_c, flip_x, flip_cx)):
            slot = lax.rem(other, 4)
            copies.append((
                remote(st_send.at[at], quad_got.at[at, quad], (b, other)),
                quad_got.at[at, slot],
            ))
        for copy, _ in copies:
            copy.start()
        quad_got[at, quad] = tile
        return copies

    def quad_sum(copies, at):
        for copy, _ in copies:
            copy.wait_recv()
        total = quad_got[at, 0]
        for k in range(1, 4):
            total = total + quad_got[at, k]
        st_mid[at] = total
        out = []
        for device in column:
            out.append(remote(st_mid.at[at], col_got.at[at, z], device))
        for copy in out:
            copy.start()
        col_got[at, z] = total
        return out

    def col_sum(copies, at):
        for copy in copies:
            copy.wait_recv()
        total = col_got[at, 0]
        for k in range(1, nz):
            total = total + col_got[at, k]
        return total

    waiting = []
    stat_copies = all_sum(st_send[0], 0)
    pl.when(has_down)(next_two.start)
    pl.when(has_across)(rows_far.start)
    rows_core.start()
    pl.when(jnp.logical_and(has_down, has_across))(corner_far.start)

    @pl.when(jnp.logical_not(has_across))
    def _():
        gp[:, far_edge] = jnp.zeros((FRAMES + 2, CH, COLS), BF16)

    @pl.when(jnp.logical_not(has_up))
    def _():
        gp[late] = jnp.zeros((2, 4, CH, COLS), BF16)

    acc[...] = jnp.zeros_like(acc)
    acts[...] = jnp.zeros_like(acts)
    stat_copies_z = quad_sum(stat_copies, 0)
    waiting += [copy for copy, _ in stat_copies] + stat_copies_z

    load_w.wait()
    for r in range(3):
        slab = jnp.concatenate(
            [wv[2 - p, 2 - q, r] for p in range(3) for q in range(3)], axis=0
        )
        wst[r * CH : (r + 1) * CH, :] = slab.astype(F32).T.astype(BF16)

    number = float(nt * ROWS * COLS * (CH // GROUPS))
    sums = group_sum(col_sum(stat_copies_z, 0), lane8) / number
    center_rows = sums
    square_rows = pltpu.roll(sums, 4, 0)
    spread_rows = lax.rsqrt(square_rows - center_rows * center_rows + EPSILON)
    both = jnp.where(row8 < 4, center_rows, pltpu.roll(spread_rows, 4, 0))
    tmat[...] = jnp.zeros((128, 128), F32)
    stats = channel_columns(both)
    load_gain.wait()
    load_shift.wait()
    tmat[0:1, 0:CH] = gain_ref[...]
    tmat[1:2, 0:CH] = shift_ref[...]
    gain_rows = jnp.broadcast_to(tmat[0:1, :], (8, 128))
    vectors = tmat[...].T[0:CH, :]
    gain, shift = vectors[:, 0:1], vectors[:, 1:2]

    for f in range(FRAMES):
        center, spread = stats[:, f : f + 1], stats[:, 4 + f : 5 + f]
        for r in range(ROWS):
            n = f * ROWS + r
            scaled = (xv[f, r].astype(F32) - center) * spread
            shaped = scaled * gain + shift
            logistic = 1.0 / (1.0 + jnp.exp(-shaped))
            active = shaped * logistic
            normed[n] = scaled
            factor[n] = logistic * (1.0 + shaped * (1.0 - logistic))
            before = jnp.where(col == 0, 0.0, pltpu.roll(active, 1, 1))
            after = jnp.where(col == COLS - 1, 0.0, pltpu.roll(active, COLS - 1, 1))
            acts[n, 0:CH] = before.astype(BF16)
            acts[n, 128 : 128 + CH] = active.astype(BF16)
            acts[n, 256 : 256 + CH] = after.astype(BF16)

    def kernel_terms(late_frames, edge_rows):
        for f in range(FRAMES):
            lo, hi = (max(f, FRAMES), f + 3) if late_frames else (f, min(f + 3, FRAMES))
            if lo >= hi:
                continue
            for r in range(ROWS):
                if edge_rows:
                    top, rows = 3 * r, 1
                else:
                    top, rows = 1, 2
                window = gp[lo:hi, top : top + rows].reshape((hi - lo) * rows * CH, COLS)
                product = lax.dot_general(
                    window, acts[f * ROWS + r], (((1,), (1,)), ((), ())),
                    preferred_element_type=F32,
                )
                height = rows * CH
                for k in range(hi - lo):
                    row = (3 * (lo + k - f) + top - r) * CH
                    acc[row : row + height] += product[k * height : (k + 1) * height]

    load_g.wait()
    kernel_terms(False, False)

    @pl.when(has_up)
    def _():
        next_two.wait_recv()
        corner_core.start()

    kernel_terms(True, False)
    rows_core.wait_recv()
    pl.when(has_across)(rows_far.wait_recv)
    kernel_terms(False, True)
    pl.when(has_up)(corner_core.wait_recv)
    pl.when(jnp.logical_and(has_up, has_across))(corner_far.wait_recv)
    kernel_terms(True, True)

    lanes = lax.broadcasted_iota(jnp.int32, (SEG, 128), 1)
    for row in range(0, 2 * TAPS + KEPT, SEG):
        slab, first = row // TAPS, row % TAPS
        value = acc[first : first + SEG, 128 * slab : 128 * slab + 128]
        k, source = row // MOVED, KEPT + row % MOVED
        if k < 3:
            extra = pltpu.roll(acc[source : source + SEG, 256:384], CH - 32 * k, 1)
            value = jnp.where(lanes < CH, value, extra)
        packed[row : row + SEG] = value
    packed[2 * TAPS + KEPT : FLAT] = jnp.zeros((FLAT - 2 * TAPS - KEPT, 128), F32)

    mine = pl.multiple_of(c * HALF, HALF)
    theirs = pl.multiple_of((1 - c) * HALF, HALF)
    core_send[...] = packed[pl.ds(theirs, HALF)].astype(BF16)
    core_copy = remote(core_send, core_got, (b, flip_c))
    core_copy.start()

    @pl.loop(0, FRAMES * ROWS)
    def _(n):
        f, r = n // ROWS, lax.rem(n, ROWS)
        window = gp[pl.ds(f, 3), pl.ds(r, 3)].reshape(TAPS, COLS)
        product = jnp.dot(wst[...], window, preferred_element_type=F32)
        after = pltpu.roll(product[0:CH], COLS - 1, 1)
        before = pltpu.roll(product[2 * CH : 3 * CH], 1, 1)
        after = jnp.where(col == COLS - 1, 0.0, after)
        before = jnp.where(col == 0, 0.0, before)
        pre[n] = (after + product[CH : 2 * CH] + before) * factor[n]

    core_copy.wait_recv()
    chip = packed[pl.ds(mine, HALF)] + core_got[...].astype(F32)
    packed[pl.ds(mine, HALF)] = chip
    plane_send[...] = chip.astype(BF16)
    plane_copies = []
    for k, (place, device) in enumerate(to_plane):
        rows = pl.ds(pl.multiple_of(place * share, share), share)
        plane_copies.append(remote(plane_send.at[rows], plane_got.at[k], device))
    for copy in plane_copies:
        copy.start()

    firsts, seconds = [], []
    for f in range(FRAMES):
        one, two = jnp.zeros((CH, 128), F32), jnp.zeros((CH, 128), F32)
        for r in range(ROWS):
            n = f * ROWS + r
            value = pre[n]
            one = one + halved(value)
            two = two + halved(value * normed[n])
        firsts.append(jnp.sum(one, axis=1, keepdims=True))
        seconds.append(jnp.sum(two, axis=1, keepdims=True))
    tmat[...] = jnp.zeros((128, 128), F32)
    st_send[1] = channel_tile(firsts + seconds)
    stat_copies = all_sum(st_send[1], 1)

    for copy in plane_copies:
        copy.wait_recv()
    part = packed[pl.ds(pl.multiple_of(mine + me * share, share), share)]
    for k in range(plane - 1):
        part = part + plane_got[k].astype(F32)
    z_send[...] = part.astype(BF16)
    z_got[z] = part.astype(BF16)
    z_copies = [remote(z_send, z_got.at[z], device) for device in column]
    for copy in z_copies:
        copy.start()

    stat_copies_z = quad_sum(stat_copies, 1)
    waiting += [copy for copy, _ in stat_copies] + stat_copies_z

    total = col_sum(stat_copies_z, 1)
    means = channel_columns(group_sum(total * gain_rows, lane8) / number)

    pairs = total + pltpu.roll(total, 2, 0)
    pairs = pairs + pltpu.roll(pairs, 1, 0)
    blk_send[...] = pairs
    blk_got[b] = pairs
    blk_copies = []
    for d in range(1, nb):
        block = lax.rem(b + d, nb)
        blk_copies.append(remote(blk_send, blk_got.at[b], (block, t)))
    for copy in blk_copies:
        copy.start()

    for copy in z_copies:
        copy.wait_recv()
    part = z_got[0].astype(F32)
    for k in range(1, nz):
        part = part + z_got[k].astype(F32)
    plane_fin[...] = (part * (1.0 / LOSS_SCALE)).astype(BF16)
    own_rows = pl.ds(pl.multiple_of(mine + me * share, share), share)
    final[own_rows] = plane_fin[...]
    spread_copies = []
    for place, device in to_plane:
        spread_copies.append(remote(plane_fin, final.at[own_rows], device))
    for copy in spread_copies:
        copy.start()
    pass_copies = [remote(plane_fin, final.at[own_rows], (b, flip_c))]
    pass_copies[0].start()

    for f in range(FRAMES):
        spread = stats[:, 4 + f : 5 + f]
        m1, m2 = means[:, f : f + 1], means[:, 4 + f : 5 + f]
        for r in range(ROWS):
            n = f * ROWS + r
            value = spread * (pre[n] * gain - m1 - normed[n] * m2)
            outv[f, r] = value.astype(BF16)
    store_x = pltpu.make_async_copy(outv, out_hbm, loc_sem.at[5])
    store_x.start()

    for copy in blk_copies:
        copy.wait_recv()
    total = blk_got[0]
    for k in range(1, nb):
        total = total + blk_got[k]
    small_ref[...] = total / LOSS_SCALE
    store_small = pltpu.make_async_copy(small_ref, small_hbm, loc_sem.at[6])
    store_small.start()

    for copy, (place, _) in zip(spread_copies, from_plane):
        copy.wait_recv()
        rows = pl.ds(pl.multiple_of(mine + place * share, share), share)
        pass_copies.append(remote(final.at[rows], final.at[rows], (b, flip_c)))
        pass_copies[-1].start()
    for copy in pass_copies:
        copy.wait_recv()

    store_fin = pltpu.make_async_copy(final, fin_hbm, loc_sem.at[7])
    store_fin.start()

    pl.when(has_down)(next_two.wait_send)
    pl.when(has_across)(rows_far.wait_send)
    pl.when(jnp.logical_and(has_down, has_across))(corner_far.wait_send)
    pl.when(has_up)(corner_core.wait_send)
    waiting += [core_copy, rows_core] + plane_copies + z_copies + blk_copies
    waiting += spread_copies + pass_copies
    for copy in waiting:
        copy.wait_send()
    store_x.wait()
    store_small.wait()
    store_fin.wait()


def unpack_body(
    out_in, fin_in, small_in, out_hbm, kg_hbm, gain_ref, shift_ref, fin_ref, small_ref, kg, sems
):
    load = pltpu.make_async_copy(fin_in, fin_ref, sems.at[4])
    load.start()
    load_small = pltpu.make_async_copy(small_in, small_ref, sems.at[5])
    load_small.start()
    store = pltpu.make_async_copy(out_in, out_hbm, sems.at[3])
    store.start()
    load_small.wait()
    gain_ref[...] = small_ref[7:8, 0:CH]
    shift_ref[...] = small_ref[3:4, 0:CH]
    load.wait()
    lanes = lax.broadcasted_iota(jnp.int32, (16, 128), 1)
    stores = []
    for p in range(3):
        for q in range(3):
            tap = ((2 - p) * 3 + 2 - q) * CH
            for r in range(2):
                kg[p, q, r] = fin_ref[r * TAPS + tap : r * TAPS + tap + CH].astype(F32)[:, 0:CH]
            for first in range(tap, tap + CH, 16):
                if first < KEPT:
                    slab = fin_ref[2 * TAPS + first : 2 * TAPS + first + 16].astype(F32)
                else:
                    slab = None
                    for k in range(3):
                        row = MOVED * k + first - KEPT
                        piece = pltpu.roll(fin_ref[row : row + 16].astype(F32), 32 + 32 * k, 1)
                        slab = piece if k == 0 else jnp.where(lanes // 32 == k, piece, slab)
                kg[p, q, 2, first - tap : first - tap + 16] = slab[:, 0:CH]
        stores.append(pltpu.make_async_copy(kg.at[p], kg_hbm.at[p], sems.at[p]))
        stores[-1].start()
    for copy in stores + [store]:
        copy.wait()


def shards(sizes, inputs, out_grads, kernel, norm_gain, norm_shift):
    nb, nz = sizes
    plane = 2 * nb
    share = HALF // plane
    copies = 5 + 2 * (3 + nz - 1) + 1 + 2 * (plane - 1) + (nz - 1) + nb - 1 + plane
    vmem = pltpu.VMEM
    in_vmem = pl.BlockSpec(memory_space=pltpu.VMEM)
    any_space = pl.BlockSpec(memory_space=pl.ANY)
    cells = FRAMES * ROWS
    out, final, small = pl.pallas_call(
        functools.partial(body, sizes),
        out_shape=(
            jax.ShapeDtypeStruct((FRAMES, ROWS, CH, COLS), BF16),
            jax.ShapeDtypeStruct((FLAT, 128), BF16),
            jax.ShapeDtypeStruct((8, 128), F32),
        ),
        in_specs=[any_space] * 5,
        out_specs=(any_space,) * 3,
        scratch_shapes=[
            vmem((1, CH), F32),
            vmem((1, CH), F32),
            vmem((FRAMES, ROWS, CH, COLS), BF16),
            vmem((8, 128), F32),
            vmem((FRAMES, ROWS, CH, COLS), BF16),
            vmem((FRAMES + 2, ROWS + 2, CH, COLS), BF16),
            vmem((3, 3, 3, CH, CH), BF16),
            vmem((3 * CH, TAPS), BF16),
            vmem((cells, CH, COLS), F32),
            vmem((cells, CH, COLS), F32),
            vmem((cells, 3 * 128, COLS), BF16),
            vmem((TAPS, 3 * 128), F32),
            vmem((cells, CH, COLS), F32),
            vmem((FLAT, 128), F32),
            vmem((HALF, 128), BF16),
            vmem((HALF, 128), BF16),
            vmem((HALF, 128), BF16),
            vmem((plane - 1, share, 128), BF16),
            vmem((share, 128), BF16),
            vmem((nz, share, 128), BF16),
            vmem((FLAT, 128), BF16),
            vmem((share, 128), BF16),
            vmem((128, 128), F32),
            vmem((2, 8, 128), F32),
            vmem((2, 4, 8, 128), F32),
            vmem((2, 8, 128), F32),
            vmem((2, nz, 8, 128), F32),
            vmem((8, 128), F32),
            vmem((nb, 8, 128), F32),
            pltpu.SemaphoreType.DMA((8,)),
            pltpu.SemaphoreType.DMA((copies,)),
            pltpu.SemaphoreType.DMA((copies,)),
        ],
        compiler_params=pltpu.CompilerParams(
            collective_id=0, has_side_effects=True, vmem_limit_bytes=60 * 1024 * 1024
        ),
    )(
        inputs, out_grads, kernel.transpose(0, 1, 3, 2, 4),
        norm_gain.reshape(1, CH), norm_shift.reshape(1, CH),
    )
    out, grad, gain, shift = pl.pallas_call(
        unpack_body,
        out_shape=(
            jax.ShapeDtypeStruct((FRAMES, ROWS, CH, COLS), BF16),
            jax.ShapeDtypeStruct((3, 3, 3, CH, CH), F32),
            jax.ShapeDtypeStruct((1, CH), F32),
            jax.ShapeDtypeStruct((1, CH), F32),
        ),
        in_specs=[any_space] * 3,
        out_specs=(any_space, any_space, in_vmem, in_vmem),
        scratch_shapes=[
            vmem((FLAT, 128), BF16),
            vmem((8, 128), F32),
            vmem((3, 3, 3, CH, CH), F32),
            pltpu.SemaphoreType.DMA((6,)),
        ],
        compiler_params=pltpu.CompilerParams(vmem_limit_bytes=60 * 1024 * 1024),
    )(out, final, small)
    return (out, grad.transpose(0, 1, 3, 2, 4), gain.reshape(CH), shift.reshape(CH))


def solution(mesh):
    sizes = (mesh.shape["block"], mesh.shape["tile"] // 4)
    placed = (P("block", "tile", None, None), P("block", "tile", None, None), P(), P(), P())
    return jax.shard_map(
        functools.partial(shards, sizes),
        mesh=mesh,
        in_specs=placed,
        out_specs=(P("block", "tile", None, None), P(), P(), P()),
        check_vma=False,
    )
```

```python
import functools

import jax
import jax.numpy as jnp
from jax import lax
from jax.experimental import pallas as pl
from jax.experimental.pallas import tpu as pltpu
from jax.sharding import PartitionSpec as P

MESH = pl.DeviceIdType.MESH
GROUPS = 32
LOSS_SCALE = 1024.0
EPSILON = 1e-06
F32 = jnp.float32
BF16 = jnp.bfloat16

FRAMES, ROWS, CH, COLS = 4, 2, 96, 256
TAPS = 9 * CH
KEPT = 240
MOVED = TAPS - KEPT
SEG = 48
FLAT = 2048
HALF = FLAT // 2


def group_sum(values, lane):
    place = lax.rem(lane, 3)
    one_up = pltpu.roll(values, 127, 1)
    two_up = pltpu.roll(values, 126, 1)
    one_down = pltpu.roll(values, 1, 1)
    two_down = pltpu.roll(values, 2, 1)
    first = jnp.where(place == 0, one_up, one_down)
    second = jnp.where(place == 2, two_down, jnp.where(place == 0, two_up, one_up))
    return values + first + second


def body(
    sizes,
    x_hbm, g_hbm, w_hbm, gain_hbm, shift_hbm,
    out_hbm, fin_hbm, small_hbm,
    gain_ref, shift_ref, outv, small_ref, xv, gp, wv, wst, factor, normed, acts, acc, pre,
    packed, core_send, core_got, plane_send, plane_got, z_send, z_got,
    final, plane_fin, tmat, st_send, core_stat, st_mid, tile_got, blk_send, blk_got,
    loc_sem, ssem, rsem,
):
    nb, nz = sizes
    ny = nb // 2
    plane = 2 * nb
    share = HALF // plane
    b = lax.axis_index("block")
    t = lax.axis_index("tile")
    nt = 4 * nz
    z = t // 4
    xh = lax.rem(t, 4) // 2
    c = lax.rem(t, 2)
    xl, y = b // ny, lax.rem(b, ny)
    flip_c = t + 1 - 2 * c
    flip_x = t + 2 - 4 * xh
    across = lax.rem(t + nt - 1 + 2 * c, nt)
    b_up = lax.rem(b + 1, nb)
    b_down = lax.rem(b + nb - 1, nb)
    me = xh * nb + b

    counter = [0]

    def remote(src, dst, device):
        i = counter[0]
        counter[0] += 1
        return pltpu.make_async_remote_copy(
            src_ref=src, dst_ref=dst, send_sem=ssem.at[i], recv_sem=rsem.at[i],
            device_id=device, device_id_type=MESH,
        )

    def plane_at(dx, dy):
        x = lax.rem(2 * xh + xl + dx, 4)
        yy = lax.rem(y + dy, ny)
        hi, lo = x // 2, lax.rem(x, 2)
        block = lo * ny + yy
        return hi * nb + block, (block, t + 2 * (hi - xh))

    steps = [(dx, dy) for dx in range(4) for dy in range(ny) if (dx, dy) != (0, 0)]
    steps.sort(key=lambda d: -min(d[0], 4 - d[0]) - min(d[1], ny - d[1]))
    to_plane = [plane_at(dx, dy) for dx, dy in steps]
    from_plane = [plane_at((4 - dx) % 4, (ny - dy) % ny) for dx, dy in steps]

    load_x = pltpu.make_async_copy(x_hbm, xv, loc_sem.at[0])
    load_g = pltpu.make_async_copy(g_hbm, gp.at[pl.ds(0, FRAMES), pl.ds(1, ROWS)], loc_sem.at[1])
    load_w = pltpu.make_async_copy(w_hbm, wv, loc_sem.at[2])
    load_gain = pltpu.make_async_copy(gain_hbm, gain_ref, loc_sem.at[3])
    load_shift = pltpu.make_async_copy(shift_hbm, shift_ref, loc_sem.at[4])
    load_x.start()
    load_g.start()
    load_gain.start()
    load_shift.start()
    load_w.start()

    barrier = pltpu.get_barrier_semaphore()
    friends = [device for _, device in to_plane]
    far_first = sorted(range(1, nz), key=lambda d: -min(d, nz - d))
    column = [(b, lax.rem(t + 4 * d, nt)) for d in far_first]
    same_core = [(b, lax.rem(flip_x + 4 * d, nt)) for d in far_first] + column
    friends += same_core
    friends += [(b, across), (b_up, across), (b_down, across), (b, flip_c)]
    same_core.append((b, flip_x))
    for device in friends:
        pl.semaphore_signal(barrier, inc=1, device_id=device, device_id_type=MESH)

    lane = lax.broadcasted_iota(jnp.int32, (CH, 128), 1)
    lane8 = lax.broadcasted_iota(jnp.int32, (8, 128), 1)
    row8 = lax.broadcasted_iota(jnp.int32, (8, 128), 0)
    col = lax.broadcasted_iota(jnp.int32, (CH, COLS), 1)
    tmat[...] = jnp.zeros((128, 128), F32)

    def channel_tile(columns):
        table = jnp.zeros((CH, 128), F32)
        for k, value in enumerate(columns):
            table = jnp.where(lane == k, value, table)
        tmat[0:CH, :] = table
        return tmat[...].T[0:8, :]

    def channel_columns(tile):
        tmat[0:8, :] = tile
        return tmat[...].T[0:CH, :]

    def halved(value):
        return value[:, 0:128] + value[:, 128:256]

    load_x.wait()
    firsts, seconds = [], []
    for f in range(FRAMES):
        one, two = jnp.zeros((CH, 128), F32), jnp.zeros((CH, 128), F32)
        for r in range(ROWS):
            value = xv[f, r].astype(F32)
            one = one + halved(value)
            two = two + halved(value * value)
        firsts.append(jnp.sum(one, axis=1, keepdims=True))
        seconds.append(jnp.sum(two, axis=1, keepdims=True))
    sums = channel_tile(firsts + seconds)

    pl.semaphore_wait(barrier, len(friends))

    has_across = jnp.where(c == 0, t > 0, t < nt - 1)
    has_down, has_up = b > 0, b < nb - 1
    four, two, late = pl.ds(0, FRAMES), pl.ds(0, 2), pl.ds(FRAMES, 2)
    core_edge, far_edge = 3 - 3 * c, 3 * c
    rows_far = remote(g_hbm.at[four, c], gp.at[four, 3 - 3 * c], (b, across))
    rows_core = remote(g_hbm.at[four, 1 - c], gp.at[four, 3 * c], (b, flip_c))
    next_two = remote(g_hbm.at[two], gp.at[late, pl.ds(1, ROWS)], (b_down, t))
    corner_far = remote(g_hbm.at[two, c], gp.at[late, 3 - 3 * c], (b_down, across))
    corner_core = remote(gp.at[late, 2 - c], gp.at[late, 3 * c], (b, flip_c))

    def all_sum(tile, at):
        st_send[at] = tile
        copy = remote(st_send.at[at], core_stat.at[at], (b, flip_c))
        copy.start()
        return copy

    def core_sum(copy, at):
        copy.wait_recv()
        total = st_send[at] + core_stat[at]
        st_mid[at] = total
        out = [remote(st_mid.at[at], tile_got.at[at, t // 2], device) for device in same_core]
        for copy in out:
            copy.start()
        tile_got[at, t // 2] = total
        return out

    def tile_sum(copies, at):
        for copy in copies:
            copy.wait_recv()
        total = tile_got[at, 0]
        for k in range(1, 2 * nz):
            total = total + tile_got[at, k]
        return total

    waiting = []
    stat_copy = all_sum(sums, 0)
    pl.when(has_down)(next_two.start)
    pl.when(has_across)(rows_far.start)
    rows_core.start()
    pl.when(jnp.logical_and(has_down, has_across))(corner_far.start)

    @pl.when(jnp.logical_not(has_across))
    def _():
        gp[:, far_edge] = jnp.zeros((FRAMES + 2, CH, COLS), BF16)

    @pl.when(jnp.logical_not(has_up))
    def _():
        gp[late] = jnp.zeros((2, 4, CH, COLS), BF16)

    acc[...] = jnp.zeros_like(acc)
    acts[...] = jnp.zeros_like(acts)
    stat_copies = core_sum(stat_copy, 0)
    waiting += [stat_copy] + stat_copies

    load_w.wait()
    for r in range(3):
        slab = jnp.concatenate(
            [wv[2 - p, 2 - q, r] for p in range(3) for q in range(3)], axis=0
        )
        wst[r * CH : (r + 1) * CH, :] = slab.astype(F32).T.astype(BF16)

    number = float(nt * ROWS * COLS * (CH // GROUPS))
    sums = group_sum(tile_sum(stat_copies, 0), lane8) / number
    center_rows = sums
    square_rows = pltpu.roll(sums, 4, 0)
    spread_rows = lax.rsqrt(square_rows - center_rows * center_rows + EPSILON)
    both = jnp.where(row8 < 4, center_rows, pltpu.roll(spread_rows, 4, 0))
    tmat[...] = jnp.zeros((128, 128), F32)
    stats = channel_columns(both)
    load_gain.wait()
    load_shift.wait()
    tmat[0:1, 0:CH] = gain_ref[...]
    tmat[1:2, 0:CH] = shift_ref[...]
    gain_rows = jnp.broadcast_to(tmat[0:1, :], (8, 128))
    vectors = tmat[...].T[0:CH, :]
    gain, shift = vectors[:, 0:1], vectors[:, 1:2]

    def kernel_terms(late_frames, edge_rows, frames=range(FRAMES)):
        for f in frames:
            lo, hi = (max(f, FRAMES), f + 3) if late_frames else (f, min(f + 3, FRAMES))
            if lo >= hi:
                continue
            for r in range(ROWS):
                if edge_rows:
                    top, rows = 3 * r, 1
                else:
                    top, rows = 1, 2
                window = gp[lo:hi, top : top + rows].reshape((hi - lo) * rows * CH, COLS)
                product = lax.dot_general(
                    window, acts[f * ROWS + r], (((1,), (1,)), ((), ())),
                    preferred_element_type=F32,
                )
                height = rows * CH
                for k in range(hi - lo):
                    row = (3 * (lo + k - f) + top - r) * CH
                    acc[row : row + height] += product[k * height : (k + 1) * height]

    @pl.when(has_up)
    def _():
        next_two.wait_recv()
        corner_core.start()

    load_g.wait()
    for f in range(FRAMES):
        center, spread = stats[:, f : f + 1], stats[:, 4 + f : 5 + f]
        for r in range(ROWS):
            n = f * ROWS + r
            scaled = (xv[f, r].astype(F32) - center) * spread
            shaped = scaled * gain + shift
            logistic = 1.0 / (1.0 + jnp.exp(-shaped))
            active = shaped * logistic
            normed[n] = scaled
            factor[n] = logistic * (1.0 + shaped * (1.0 - logistic))
            before = jnp.where(col == 0, 0.0, pltpu.roll(active, 1, 1))
            after = jnp.where(col == COLS - 1, 0.0, pltpu.roll(active, COLS - 1, 1))
            acts[n, 0:CH] = before.astype(BF16)
            acts[n, 128 : 128 + CH] = active.astype(BF16)
            acts[n, 256 : 256 + CH] = after.astype(BF16)
        kernel_terms(False, False, (f,))

    kernel_terms(True, False)
    rows_core.wait_recv()
    pl.when(has_across)(rows_far.wait_recv)
    kernel_terms(False, True)
    pl.when(has_up)(corner_core.wait_recv)
    pl.when(jnp.logical_and(has_up, has_across))(corner_far.wait_recv)
    kernel_terms(True, True)

    lanes = lax.broadcasted_iota(jnp.int32, (SEG, 128), 1)
    for row in range(0, 2 * TAPS + KEPT, SEG):
        slab, first = row // TAPS, row % TAPS
        value = acc[first : first + SEG, 128 * slab : 128 * slab + 128]
        k, source = row // MOVED, KEPT + row % MOVED
        if k < 3:
            extra = pltpu.roll(acc[source : source + SEG, 256:384], CH - 32 * k, 1)
            value = jnp.where(lanes < CH, value, extra)
        packed[row : row + SEG] = value
    packed[2 * TAPS + KEPT : FLAT] = jnp.zeros((FLAT - 2 * TAPS - KEPT, 128), F32)

    mine = pl.multiple_of(c * HALF, HALF)
    theirs = pl.multiple_of((1 - c) * HALF, HALF)
    core_send[...] = packed[pl.ds(theirs, HALF)].astype(BF16)
    core_copy = remote(core_send, core_got, (b, flip_c))
    core_copy.start()

    @pl.loop(0, FRAMES * ROWS)
    def _(n):
        f, r = n // ROWS, lax.rem(n, ROWS)
        window = gp[pl.ds(f, 3), pl.ds(r, 3)].reshape(TAPS, COLS)
        product = jnp.dot(wst[...], window, preferred_element_type=F32)
        after = pltpu.roll(product[0:CH], COLS - 1, 1)
        before = pltpu.roll(product[2 * CH : 3 * CH], 1, 1)
        after = jnp.where(col == COLS - 1, 0.0, after)
        before = jnp.where(col == 0, 0.0, before)
        pre[n] = (after + product[CH : 2 * CH] + before) * factor[n]

    core_copy.wait_recv()
    chip = packed[pl.ds(mine, HALF)] + core_got[...].astype(F32)
    packed[pl.ds(mine, HALF)] = chip
    plane_send[...] = chip.astype(BF16)
    plane_copies = []
    for k, (place, device) in enumerate(to_plane):
        rows = pl.ds(pl.multiple_of(place * share, share), share)
        plane_copies.append(remote(plane_send.at[rows], plane_got.at[k], device))
    for copy in plane_copies:
        copy.start()

    firsts, seconds = [], []
    for f in range(FRAMES):
        one, two = jnp.zeros((CH, 128), F32), jnp.zeros((CH, 128), F32)
        for r in range(ROWS):
            n = f * ROWS + r
            value = pre[n]
            one = one + halved(value)
            two = two + halved(value * normed[n])
        firsts.append(jnp.sum(one, axis=1, keepdims=True))
        seconds.append(jnp.sum(two, axis=1, keepdims=True))
    tmat[...] = jnp.zeros((128, 128), F32)
    stat_copy = all_sum(channel_tile(firsts + seconds), 1)

    for copy in plane_copies:
        copy.wait_recv()
    part = packed[pl.ds(pl.multiple_of(mine + me * share, share), share)]
    for k in range(plane - 1):
        part = part + plane_got[k].astype(F32)
    z_send[...] = part.astype(BF16)
    z_got[z] = part.astype(BF16)
    z_copies = [remote(z_send, z_got.at[z], device) for device in column]
    for copy in z_copies:
        copy.start()

    stat_copies = core_sum(stat_copy, 1)
    waiting += [stat_copy] + stat_copies

    total = tile_sum(stat_copies, 1)
    means = channel_columns(group_sum(total * gain_rows, lane8) / number)

    pairs = total + pltpu.roll(total, 2, 0)
    pairs = pairs + pltpu.roll(pairs, 1, 0)
    blk_send[...] = pairs
    blk_got[b] = pairs
    blk_copies = []
    for d in range(1, nb):
        block = lax.rem(b + d, nb)
        blk_copies.append(remote(blk_send, blk_got.at[b], (block, t)))
    for copy in blk_copies:
        copy.start()

    for copy in z_copies:
        copy.wait_recv()
    part = z_got[0].astype(F32)
    for k in range(1, nz):
        part = part + z_got[k].astype(F32)
    plane_fin[...] = (part * (1.0 / LOSS_SCALE)).astype(BF16)
    own_rows = pl.ds(pl.multiple_of(mine + me * share, share), share)
    final[own_rows] = plane_fin[...]
    spread_copies = []
    for place, device in to_plane:
        spread_copies.append(remote(plane_fin, final.at[own_rows], device))
    for copy in spread_copies:
        copy.start()
    pass_copies = [remote(plane_fin, final.at[own_rows], (b, flip_c))]
    pass_copies[0].start()

    for f in range(FRAMES):
        spread = stats[:, 4 + f : 5 + f]
        m1, m2 = means[:, f : f + 1], means[:, 4 + f : 5 + f]
        for r in range(ROWS):
            n = f * ROWS + r
            value = spread * (pre[n] * gain - m1 - normed[n] * m2)
            outv[f, r] = value.astype(BF16)
    store_x = pltpu.make_async_copy(outv, out_hbm, loc_sem.at[5])
    store_x.start()

    for copy in blk_copies:
        copy.wait_recv()
    total = blk_got[0]
    for k in range(1, nb):
        total = total + blk_got[k]
    small_ref[...] = total / LOSS_SCALE
    store_small = pltpu.make_async_copy(small_ref, small_hbm, loc_sem.at[6])
    store_small.start()

    for copy, (place, _) in reversed(list(zip(spread_copies, from_plane))):
        copy.wait_recv()
        rows = pl.ds(pl.multiple_of(mine + place * share, share), share)
        pass_copies.append(remote(final.at[rows], final.at[rows], (b, flip_c)))
        pass_copies[-1].start()
    for copy in pass_copies:
        copy.wait_recv()

    store_fin = pltpu.make_async_copy(final, fin_hbm, loc_sem.at[7])
    store_fin.start()

    pl.when(has_down)(next_two.wait_send)
    pl.when(has_across)(rows_far.wait_send)
    pl.when(jnp.logical_and(has_down, has_across))(corner_far.wait_send)
    pl.when(has_up)(corner_core.wait_send)
    waiting += [core_copy, rows_core] + plane_copies + z_copies + blk_copies
    waiting += spread_copies + pass_copies
    for copy in waiting:
        copy.wait_send()
    store_x.wait()
    store_small.wait()
    store_fin.wait()


def unpack_body(
    out_in, fin_in, small_in, out_hbm, kg_hbm, gain_ref, shift_ref,
    out_ref, fin_ref, small_ref, kg, sems,
):
    load = pltpu.make_async_copy(fin_in, fin_ref, sems.at[4])
    load.start()
    load_small = pltpu.make_async_copy(small_in, small_ref, sems.at[5])
    load_small.start()
    load_out = pltpu.make_async_copy(out_in, out_ref, sems.at[6])
    load_out.start()
    load_small.wait()
    gain_ref[...] = small_ref[7:8, 0:CH]
    shift_ref[...] = small_ref[3:4, 0:CH]
    load_out.wait()
    store = pltpu.make_async_copy(out_ref, out_hbm, sems.at[3])
    store.start()
    load.wait()
    lanes = lax.broadcasted_iota(jnp.int32, (16, 128), 1)
    stores = []
    for p in range(3):
        for q in range(3):
            tap = ((2 - p) * 3 + 2 - q) * CH
            for r in range(2):
                kg[p, q, r] = fin_ref[r * TAPS + tap : r * TAPS + tap + CH].astype(F32)[:, 0:CH]
            for first in range(tap, tap + CH, 16):
                if first < KEPT:
                    slab = fin_ref[2 * TAPS + first : 2 * TAPS + first + 16].astype(F32)
                else:
                    slab = None
                    for k in range(3):
                        row = MOVED * k + first - KEPT
                        piece = pltpu.roll(fin_ref[row : row + 16].astype(F32), 32 + 32 * k, 1)
                        slab = piece if k == 0 else jnp.where(lanes // 32 == k, piece, slab)
                kg[p, q, 2, first - tap : first - tap + 16] = slab[:, 0:CH]
        stores.append(pltpu.make_async_copy(kg.at[p], kg_hbm.at[p], sems.at[p]))
        stores[-1].start()
    for copy in stores + [store]:
        copy.wait()


def shards(sizes, inputs, out_grads, kernel, norm_gain, norm_shift):
    nb, nz = sizes
    plane = 2 * nb
    share = HALF // plane
    copies = 5 + 2 * (1 + 2 * nz - 1) + 1 + 2 * (plane - 1) + (nz - 1) + nb - 1 + plane
    vmem = pltpu.VMEM
    in_vmem = pl.BlockSpec(memory_space=pltpu.VMEM)
    any_space = pl.BlockSpec(memory_space=pl.ANY)
    cells = FRAMES * ROWS
    out, final, small = pl.pallas_call(
        functools.partial(body, sizes),
        out_shape=(
            jax.ShapeDtypeStruct((FRAMES, ROWS, CH, COLS), BF16),
            jax.ShapeDtypeStruct((FLAT, 128), BF16),
            jax.ShapeDtypeStruct((8, 128), F32),
        ),
        in_specs=[any_space] * 5,
        out_specs=(any_space,) * 3,
        scratch_shapes=[
            vmem((1, CH), F32),
            vmem((1, CH), F32),
            vmem((FRAMES, ROWS, CH, COLS), BF16),
            vmem((8, 128), F32),
            vmem((FRAMES, ROWS, CH, COLS), BF16),
            vmem((FRAMES + 2, ROWS + 2, CH, COLS), BF16),
            vmem((3, 3, 3, CH, CH), BF16),
            vmem((3 * CH, TAPS), BF16),
            vmem((cells, CH, COLS), F32),
            vmem((cells, CH, COLS), F32),
            vmem((cells, 3 * 128, COLS), BF16),
            vmem((TAPS, 3 * 128), F32),
            vmem((cells, CH, COLS), F32),
            vmem((FLAT, 128), F32),
            vmem((HALF, 128), BF16),
            vmem((HALF, 128), BF16),
            vmem((HALF, 128), BF16),
            vmem((plane - 1, share, 128), BF16),
            vmem((share, 128), BF16),
            vmem((nz, share, 128), BF16),
            vmem((FLAT, 128), BF16),
            vmem((share, 128), BF16),
            vmem((128, 128), F32),
            vmem((2, 8, 128), F32),
            vmem((2, 8, 128), F32),
            vmem((2, 8, 128), F32),
            vmem((2, 2 * nz, 8, 128), F32),
            vmem((8, 128), F32),
            vmem((nb, 8, 128), F32),
            pltpu.SemaphoreType.DMA((8,)),
            pltpu.SemaphoreType.DMA((copies,)),
            pltpu.SemaphoreType.DMA((copies,)),
        ],
        compiler_params=pltpu.CompilerParams(
            collective_id=0, has_side_effects=True, vmem_limit_bytes=60 * 1024 * 1024
        ),
    )(
        inputs, out_grads, kernel.transpose(0, 1, 3, 2, 4),
        norm_gain.reshape(1, CH), norm_shift.reshape(1, CH),
    )
    out, grad, gain, shift = pl.pallas_call(
        unpack_body,
        out_shape=(
            jax.ShapeDtypeStruct((FRAMES, ROWS, CH, COLS), BF16),
            jax.ShapeDtypeStruct((3, 3, 3, CH, CH), F32),
            jax.ShapeDtypeStruct((1, CH), F32),
            jax.ShapeDtypeStruct((1, CH), F32),
        ),
        in_specs=[any_space] * 3,
        out_specs=(any_space, any_space, in_vmem, in_vmem),
        scratch_shapes=[
            vmem((FRAMES, ROWS, CH, COLS), BF16),
            vmem((FLAT, 128), BF16),
            vmem((8, 128), F32),
            vmem((3, 3, 3, CH, CH), F32),
            pltpu.SemaphoreType.DMA((7,)),
        ],
        compiler_params=pltpu.CompilerParams(vmem_limit_bytes=60 * 1024 * 1024),
    )(out, final, small)
    return (out, grad.transpose(0, 1, 3, 2, 4), gain.reshape(CH), shift.reshape(CH))


def solution(mesh):
    sizes = (mesh.shape["block"], mesh.shape["tile"] // 4)
    placed = (P("block", "tile", None, None), P("block", "tile", None, None), P(), P(), P())
    return jax.shard_map(
        functools.partial(shards, sizes),
        mesh=mesh,
        in_specs=placed,
        out_specs=(P("block", "tile", None, None), P(), P(), P()),
        check_vma=False,
    )
```

```python
import functools

import jax
import jax.numpy as jnp
from jax import lax
from jax.experimental import pallas as pl
from jax.experimental.pallas import tpu as pltpu
from jax.sharding import PartitionSpec as P

MESH = pl.DeviceIdType.MESH
GROUPS = 32
LOSS_SCALE = 1024.0
EPSILON = 1e-06
F32 = jnp.float32
BF16 = jnp.bfloat16

FRAMES, ROWS, CH, COLS = 4, 2, 96, 256
TAPS = 9 * CH
KEPT = 240
MOVED = TAPS - KEPT
SEG = 48
FLAT = 2048
HALF = FLAT // 2


def group_sum(values, lane):
    place = lax.rem(lane, 3)
    one_up = pltpu.roll(values, 127, 1)
    two_up = pltpu.roll(values, 126, 1)
    one_down = pltpu.roll(values, 1, 1)
    two_down = pltpu.roll(values, 2, 1)
    first = jnp.where(place == 0, one_up, one_down)
    second = jnp.where(place == 2, two_down, jnp.where(place == 0, two_up, one_up))
    return values + first + second


def body(
    sizes,
    x_hbm, g_hbm, w_hbm, gain_hbm, shift_hbm,
    out_hbm, fin_hbm, small_hbm,
    gain_ref, shift_ref, outv, small_ref, xv, gp, wv, wst, factor, normed, acts, acc, pre,
    packed, core_send, core_got, plane_send, plane_got, z_send, z_got,
    final, plane_fin, tmat, st_send, quad_got, st_mid, col_got, blk_send, blk_got,
    loc_sem, ssem, rsem,
):
    nb, nz = sizes
    ny = nb // 2
    plane = 2 * nb
    share = HALF // plane
    b = lax.axis_index("block")
    t = lax.axis_index("tile")
    nt = 4 * nz
    z = t // 4
    xh = lax.rem(t, 4) // 2
    c = lax.rem(t, 2)
    xl, y = b // ny, lax.rem(b, ny)
    flip_c = t + 1 - 2 * c
    flip_x = t + 2 - 4 * xh
    flip_cx = flip_c + 2 - 4 * xh
    across = lax.rem(t + nt - 1 + 2 * c, nt)
    b_up = lax.rem(b + 1, nb)
    b_down = lax.rem(b + nb - 1, nb)
    me = xh * nb + b

    counter = [0]

    def remote(src, dst, device):
        i = counter[0]
        counter[0] += 1
        return pltpu.make_async_remote_copy(
            src_ref=src, dst_ref=dst, send_sem=ssem.at[i], recv_sem=rsem.at[i],
            device_id=device, device_id_type=MESH,
        )

    def plane_at(dx, dy):
        x = lax.rem(2 * xh + xl + dx, 4)
        yy = lax.rem(y + dy, ny)
        hi, lo = x // 2, lax.rem(x, 2)
        block = lo * ny + yy
        return hi * nb + block, (block, t + 2 * (hi - xh))

    steps = [(dx, dy) for dx in range(4) for dy in range(ny) if (dx, dy) != (0, 0)]
    steps.sort(key=lambda d: -min(d[0], 4 - d[0]) - min(d[1], ny - d[1]))
    to_plane = [plane_at(dx, dy) for dx, dy in steps]
    from_plane = [plane_at((4 - dx) % 4, (ny - dy) % ny) for dx, dy in steps]

    load_x = pltpu.make_async_copy(x_hbm, xv, loc_sem.at[0])
    load_g = pltpu.make_async_copy(g_hbm, gp.at[pl.ds(0, FRAMES), pl.ds(1, ROWS)], loc_sem.at[1])
    load_w = pltpu.make_async_copy(w_hbm, wv, loc_sem.at[2])
    load_gain = pltpu.make_async_copy(gain_hbm, gain_ref, loc_sem.at[3])
    load_shift = pltpu.make_async_copy(shift_hbm, shift_ref, loc_sem.at[4])
    load_x.start()
    load_g.start()
    load_gain.start()
    load_shift.start()
    load_w.start()

    barrier = pltpu.get_barrier_semaphore()
    friends = [device for _, device in to_plane]
    far_first = sorted(range(1, nz), key=lambda d: -min(d, nz - d))
    column = [(b, lax.rem(t + 4 * d, nt)) for d in far_first]
    friends += column
    friends += [(b, across), (b_up, across), (b_down, across), (b, flip_c), (b, flip_cx)]
    for device in friends:
        pl.semaphore_signal(barrier, inc=1, device_id=device, device_id_type=MESH)

    lane = lax.broadcasted_iota(jnp.int32, (CH, 128), 1)
    lane8 = lax.broadcasted_iota(jnp.int32, (8, 128), 1)
    row8 = lax.broadcasted_iota(jnp.int32, (8, 128), 0)
    col = lax.broadcasted_iota(jnp.int32, (CH, COLS), 1)
    tmat[...] = jnp.zeros((128, 128), F32)

    def channel_tile(columns):
        table = jnp.zeros((CH, 128), F32)
        for k, value in enumerate(columns):
            table = jnp.where(lane == k, value, table)
        tmat[0:CH, :] = table
        return tmat[...].T[0:8, :]

    def channel_columns(tile):
        tmat[0:8, :] = tile
        return tmat[...].T[0:CH, :]

    def halved(value):
        return value[:, 0:128] + value[:, 128:256]

    load_x.wait()
    firsts, seconds = [], []
    for f in range(FRAMES):
        one, two = jnp.zeros((CH, 128), F32), jnp.zeros((CH, 128), F32)
        for r in range(ROWS):
            value = xv[f, r].astype(F32)
            one = one + halved(value)
            two = two + halved(value * value)
        firsts.append(jnp.sum(one, axis=1, keepdims=True))
        seconds.append(jnp.sum(two, axis=1, keepdims=True))
    st_send[0] = channel_tile(firsts + seconds)

    pl.semaphore_wait(barrier, len(friends))

    has_across = jnp.where(c == 0, t > 0, t < nt - 1)
    has_down, has_up = b > 0, b < nb - 1
    four, two, late = pl.ds(0, FRAMES), pl.ds(0, 2), pl.ds(FRAMES, 2)
    core_edge, far_edge = 3 - 3 * c, 3 * c
    rows_far = remote(g_hbm.at[four, c], gp.at[four, 3 - 3 * c], (b, across))
    rows_core = remote(g_hbm.at[four, 1 - c], gp.at[four, 3 * c], (b, flip_c))
    next_two = remote(g_hbm.at[two], gp.at[late, pl.ds(1, ROWS)], (b_down, t))
    corner_far = remote(g_hbm.at[two, c], gp.at[late, 3 - 3 * c], (b_down, across))
    corner_core = remote(gp.at[late, 2 - c], gp.at[late, 3 * c], (b, flip_c))

    def all_sum(tile, at):
        quad = 2 * xh + c
        copies = []
        for k, other in enumerate((flip_c, flip_x, flip_cx)):
            slot = lax.rem(other, 4)
            copies.append((
                remote(st_send.at[at], quad_got.at[at, quad], (b, other)),
                quad_got.at[at, slot],
            ))
        for copy, _ in copies:
            copy.start()
        quad_got[at, quad] = tile
        return copies

    def quad_sum(copies, at):
        for copy, _ in copies:
            copy.wait_recv()
        total = quad_got[at, 0]
        for k in range(1, 4):
            total = total + quad_got[at, k]
        st_mid[at] = total
        out = []
        for device in column:
            out.append(remote(st_mid.at[at], col_got.at[at, z], device))
        for copy in out:
            copy.start()
        col_got[at, z] = total
        return out

    def col_sum(copies, at):
        for copy in copies:
            copy.wait_recv()
        total = col_got[at, 0]
        for k in range(1, nz):
            total = total + col_got[at, k]
        return total

    waiting = []
    stat_copies = all_sum(st_send[0], 0)
    pl.when(has_down)(next_two.start)
    pl.when(has_across)(rows_far.start)
    rows_core.start()

    @pl.when(jnp.logical_not(has_across))
    def _():
        gp[:, far_edge] = jnp.zeros((FRAMES + 2, CH, COLS), BF16)

    @pl.when(jnp.logical_not(has_up))
    def _():
        gp[late] = jnp.zeros((2, 4, CH, COLS), BF16)

    acc[...] = jnp.zeros_like(acc)
    acts[...] = jnp.zeros_like(acts)
    stat_copies_z = quad_sum(stat_copies, 0)
    pl.when(jnp.logical_and(has_down, has_across))(corner_far.start)
    waiting += [copy for copy, _ in stat_copies] + stat_copies_z

    load_w.wait()
    for r in range(3):
        slab = jnp.concatenate(
            [wv[2 - p, 2 - q, r] for p in range(3) for q in range(3)], axis=0
        )
        wst[r * CH : (r + 1) * CH, :] = slab.astype(F32).T.astype(BF16)

    number = float(nt * ROWS * COLS * (CH // GROUPS))
    sums = group_sum(col_sum(stat_copies_z, 0), lane8) / number
    center_rows = sums
    square_rows = pltpu.roll(sums, 4, 0)
    spread_rows = lax.rsqrt(square_rows - center_rows * center_rows + EPSILON)
    both = jnp.where(row8 < 4, center_rows, pltpu.roll(spread_rows, 4, 0))
    tmat[...] = jnp.zeros((128, 128), F32)
    stats = channel_columns(both)
    load_gain.wait()
    load_shift.wait()
    tmat[0:1, 0:CH] = gain_ref[...]
    tmat[1:2, 0:CH] = shift_ref[...]
    gain_rows = jnp.broadcast_to(tmat[0:1, :], (8, 128))
    vectors = tmat[...].T[0:CH, :]
    gain, shift = vectors[:, 0:1], vectors[:, 1:2]

    def kernel_terms(late_frames, edge_rows, frames=range(FRAMES)):
        for f in frames:
            lo, hi = (max(f, FRAMES), f + 3) if late_frames else (f, min(f + 3, FRAMES))
            if lo >= hi:
                continue
            for r in range(ROWS):
                if edge_rows:
                    top, rows = 3 * r, 1
                else:
                    top, rows = 1, 2
                window = gp[lo:hi, top : top + rows].reshape((hi - lo) * rows * CH, COLS)
                product = lax.dot_general(
                    window, acts[f * ROWS + r], (((1,), (1,)), ((), ())),
                    preferred_element_type=F32,
                )
                height = rows * CH
                for k in range(hi - lo):
                    row = (3 * (lo + k - f) + top - r) * CH
                    acc[row : row + height] += product[k * height : (k + 1) * height]

    @pl.when(has_up)
    def _():
        next_two.wait_recv()
        corner_core.start()

    load_g.wait()
    for f in range(FRAMES):
        center, spread = stats[:, f : f + 1], stats[:, 4 + f : 5 + f]
        for r in range(ROWS):
            n = f * ROWS + r
            scaled = (xv[f, r].astype(F32) - center) * spread
            shaped = scaled * gain + shift
            logistic = 1.0 / (1.0 + jnp.exp(-shaped))
            active = shaped * logistic
            normed[n] = scaled
            factor[n] = logistic * (1.0 + shaped * (1.0 - logistic))
            before = jnp.where(col == 0, 0.0, pltpu.roll(active, 1, 1))
            after = jnp.where(col == COLS - 1, 0.0, pltpu.roll(active, COLS - 1, 1))
            acts[n, 0:CH] = before.astype(BF16)
            acts[n, 128 : 128 + CH] = active.astype(BF16)
            acts[n, 256 : 256 + CH] = after.astype(BF16)
        kernel_terms(False, False, (f,))

    kernel_terms(True, False)
    rows_core.wait_recv()
    pl.when(has_across)(rows_far.wait_recv)
    kernel_terms(False, True)
    pl.when(has_up)(corner_core.wait_recv)
    pl.when(jnp.logical_and(has_up, has_across))(corner_far.wait_recv)
    kernel_terms(True, True)

    lanes = lax.broadcasted_iota(jnp.int32, (SEG, 128), 1)
    for row in range(0, 2 * TAPS + KEPT, SEG):
        slab, first = row // TAPS, row % TAPS
        value = acc[first : first + SEG, 128 * slab : 128 * slab + 128]
        k, source = row // MOVED, KEPT + row % MOVED
        if k < 3:
            extra = pltpu.roll(acc[source : source + SEG, 256:384], CH - 32 * k, 1)
            value = jnp.where(lanes < CH, value, extra)
        packed[row : row + SEG] = value
    packed[2 * TAPS + KEPT : FLAT] = jnp.zeros((FLAT - 2 * TAPS - KEPT, 128), F32)

    mine = pl.multiple_of(c * HALF, HALF)
    theirs = pl.multiple_of((1 - c) * HALF, HALF)
    core_send[...] = packed[pl.ds(theirs, HALF)].astype(BF16)
    core_copy = remote(core_send, core_got, (b, flip_c))
    core_copy.start()

    def act_grad(n):
        f, r = n // ROWS, lax.rem(n, ROWS)
        window = gp[pl.ds(f, 3), pl.ds(r, 3)].reshape(TAPS, COLS)
        product = jnp.dot(wst[...], window, preferred_element_type=F32)
        after = pltpu.roll(product[0:CH], COLS - 1, 1)
        before = pltpu.roll(product[2 * CH : 3 * CH], 1, 1)
        after = jnp.where(col == COLS - 1, 0.0, after)
        before = jnp.where(col == 0, 0.0, before)
        pre[n] = (after + product[CH : 2 * CH] + before) * factor[n]

    pl.loop(0, 4)(act_grad)
    core_copy.wait_recv()
    chip = packed[pl.ds(mine, HALF)] + core_got[...].astype(F32)
    packed[pl.ds(mine, HALF)] = chip
    plane_send[...] = chip.astype(BF16)
    plane_copies = []
    for k, (place, device) in enumerate(to_plane):
        rows = pl.ds(pl.multiple_of(place * share, share), share)
        plane_copies.append(remote(plane_send.at[rows], plane_got.at[k], device))
    for copy in plane_copies:
        copy.start()

    pl.loop(4, FRAMES * ROWS)(act_grad)

    firsts, seconds = [], []
    for f in range(FRAMES):
        one, two = jnp.zeros((CH, 128), F32), jnp.zeros((CH, 128), F32)
        for r in range(ROWS):
            n = f * ROWS + r
            value = pre[n]
            one = one + halved(value)
            two = two + halved(value * normed[n])
        firsts.append(jnp.sum(one, axis=1, keepdims=True))
        seconds.append(jnp.sum(two, axis=1, keepdims=True))
    tmat[...] = jnp.zeros((128, 128), F32)
    st_send[1] = channel_tile(firsts + seconds)
    stat_copies = all_sum(st_send[1], 1)

    for copy in plane_copies:
        copy.wait_recv()
    part = packed[pl.ds(pl.multiple_of(mine + me * share, share), share)]
    for k in range(plane - 1):
        part = part + plane_got[k].astype(F32)
    z_send[...] = part.astype(BF16)
    z_got[z] = part.astype(BF16)
    z_copies = [remote(z_send, z_got.at[z], device) for device in column]
    for copy in z_copies:
        copy.start()

    stat_copies_z = quad_sum(stat_copies, 1)
    waiting += [copy for copy, _ in stat_copies] + stat_copies_z

    for copy in z_copies:
        copy.wait_recv()
    part = z_got[0].astype(F32)
    for k in range(1, nz):
        part = part + z_got[k].astype(F32)
    plane_fin[...] = (part * (1.0 / LOSS_SCALE)).astype(BF16)
    own_rows = pl.ds(pl.multiple_of(mine + me * share, share), share)
    final[own_rows] = plane_fin[...]
    spread_copies = []
    for place, device in to_plane:
        spread_copies.append(remote(plane_fin, final.at[own_rows], device))
    for copy in spread_copies:
        copy.start()
    pass_copies = [remote(plane_fin, final.at[own_rows], (b, flip_c))]
    pass_copies[0].start()

    total = col_sum(stat_copies_z, 1)
    means = channel_columns(group_sum(total * gain_rows, lane8) / number)

    pairs = total + pltpu.roll(total, 2, 0)
    pairs = pairs + pltpu.roll(pairs, 1, 0)
    blk_send[...] = pairs
    blk_got[b] = pairs
    blk_copies = []
    for d in range(1, nb):
        block = lax.rem(b + d, nb)
        blk_copies.append(remote(blk_send, blk_got.at[b], (block, t)))
    for copy in blk_copies:
        copy.start()

    for f in range(FRAMES):
        spread = stats[:, 4 + f : 5 + f]
        m1, m2 = means[:, f : f + 1], means[:, 4 + f : 5 + f]
        for r in range(ROWS):
            n = f * ROWS + r
            value = spread * (pre[n] * gain - m1 - normed[n] * m2)
            outv[f, r] = value.astype(BF16)
    store_x = pltpu.make_async_copy(outv, out_hbm, loc_sem.at[5])
    store_x.start()

    for copy, (place, _) in reversed(list(zip(spread_copies, from_plane))):
        copy.wait_recv()
        rows = pl.ds(pl.multiple_of(mine + place * share, share), share)
        pass_copies.append(remote(final.at[rows], final.at[rows], (b, flip_c)))
        pass_copies[-1].start()
    for copy in blk_copies:
        copy.wait_recv()
    total = blk_got[0]
    for k in range(1, nb):
        total = total + blk_got[k]
    small_ref[...] = total / LOSS_SCALE
    store_small = pltpu.make_async_copy(small_ref, small_hbm, loc_sem.at[6])
    store_small.start()

    for copy in pass_copies:
        copy.wait_recv()

    store_fin = pltpu.make_async_copy(final, fin_hbm, loc_sem.at[7])
    store_fin.start()

    pl.when(has_down)(next_two.wait_send)
    pl.when(has_across)(rows_far.wait_send)
    pl.when(jnp.logical_and(has_down, has_across))(corner_far.wait_send)
    pl.when(has_up)(corner_core.wait_send)
    waiting += [core_copy, rows_core] + plane_copies + z_copies + blk_copies
    waiting += spread_copies + pass_copies
    for copy in waiting:
        copy.wait_send()
    store_x.wait()
    store_small.wait()
    store_fin.wait()


def unpack_body(
    out_in, fin_in, small_in, out_hbm, kg_hbm, gain_ref, shift_ref,
    out_ref, fin_ref, small_ref, kg, sems,
):
    bounds = (0, TAPS, 2 * TAPS, FLAT)
    loads = []
    for k in range(3):
        rows = pl.ds(bounds[k], bounds[k + 1] - bounds[k])
        loads.append(pltpu.make_async_copy(fin_in.at[rows], fin_ref.at[rows], sems.at[k]))
        loads[k].start()
    load_out = pltpu.make_async_copy(out_in, out_ref, sems.at[3])
    load_out.start()
    load_small = pltpu.make_async_copy(small_in, small_ref, sems.at[4])
    load_small.start()
    lanes = lax.broadcasted_iota(jnp.int32, (16, 128), 1)
    stores = []
    for r in range(3):
        loads[r].wait()
        for p in range(3):
            for q in range(3):
                tap = ((2 - p) * 3 + 2 - q) * CH
                if r < 2:
                    slab = fin_ref[r * TAPS + tap : r * TAPS + tap + CH].astype(F32)
                    kg[p, q, r] = slab[:, 0:CH]
                    continue
                for first in range(tap, tap + CH, 16):
                    if first < KEPT:
                        slab = fin_ref[2 * TAPS + first : 2 * TAPS + first + 16].astype(F32)
                    else:
                        slab = None
                        for k in range(3):
                            row = MOVED * k + first - KEPT
                            piece = fin_ref[row : row + 16].astype(F32)
                            piece = pltpu.roll(piece, 32 + 32 * k, 1)
                            slab = piece if k == 0 else jnp.where(lanes // 32 == k, piece, slab)
                    kg[p, q, 2, first - tap : first - tap + 16] = slab[:, 0:CH]
        store = pltpu.make_async_copy(kg.at[:, :, r], kg_hbm.at[:, :, r], sems.at[5 + r])
        store.start()
        stores.append(store)
        if r == 0:
            load_out.wait()
            stores.append(pltpu.make_async_copy(out_ref, out_hbm, sems.at[8]))
            stores[-1].start()
    load_small.wait()
    gain_ref[...] = small_ref[7:8, 0:CH]
    shift_ref[...] = small_ref[3:4, 0:CH]
    for copy in stores:
        copy.wait()


def shards(sizes, inputs, out_grads, kernel, norm_gain, norm_shift):
    nb, nz = sizes
    plane = 2 * nb
    share = HALF // plane
    copies = 5 + 2 * (3 + nz - 1) + 1 + 2 * (plane - 1) + (nz - 1) + nb - 1 + plane
    vmem = pltpu.VMEM
    in_vmem = pl.BlockSpec(memory_space=pltpu.VMEM)
    any_space = pl.BlockSpec(memory_space=pl.ANY)
    cells = FRAMES * ROWS
    out, final, small = pl.pallas_call(
        functools.partial(body, sizes),
        out_shape=(
            jax.ShapeDtypeStruct((FRAMES, ROWS, CH, COLS), BF16),
            jax.ShapeDtypeStruct((FLAT, 128), BF16),
            jax.ShapeDtypeStruct((8, 128), F32),
        ),
        in_specs=[any_space] * 5,
        out_specs=(any_space,) * 3,
        scratch_shapes=[
            vmem((1, CH), F32),
            vmem((1, CH), F32),
            vmem((FRAMES, ROWS, CH, COLS), BF16),
            vmem((8, 128), F32),
            vmem((FRAMES, ROWS, CH, COLS), BF16),
            vmem((FRAMES + 2, ROWS + 2, CH, COLS), BF16),
            vmem((3, 3, 3, CH, CH), BF16),
            vmem((3 * CH, TAPS), BF16),
            vmem((cells, CH, COLS), F32),
            vmem((cells, CH, COLS), F32),
            vmem((cells, 3 * 128, COLS), BF16),
            vmem((TAPS, 3 * 128), F32),
            vmem((cells, CH, COLS), F32),
            vmem((FLAT, 128), F32),
            vmem((HALF, 128), BF16),
            vmem((HALF, 128), BF16),
            vmem((HALF, 128), BF16),
            vmem((plane - 1, share, 128), BF16),
            vmem((share, 128), BF16),
            vmem((nz, share, 128), BF16),
            vmem((FLAT, 128), BF16),
            vmem((share, 128), BF16),
            vmem((128, 128), F32),
            vmem((2, 8, 128), F32),
            vmem((2, 4, 8, 128), F32),
            vmem((2, 8, 128), F32),
            vmem((2, nz, 8, 128), F32),
            vmem((8, 128), F32),
            vmem((nb, 8, 128), F32),
            pltpu.SemaphoreType.DMA((8,)),
            pltpu.SemaphoreType.DMA((copies,)),
            pltpu.SemaphoreType.DMA((copies,)),
        ],
        compiler_params=pltpu.CompilerParams(
            collective_id=0, has_side_effects=True, vmem_limit_bytes=60 * 1024 * 1024
        ),
    )(
        inputs, out_grads, kernel.transpose(0, 1, 3, 2, 4),
        norm_gain.reshape(1, CH), norm_shift.reshape(1, CH),
    )
    out, grad, gain, shift = pl.pallas_call(
        unpack_body,
        out_shape=(
            jax.ShapeDtypeStruct((FRAMES, ROWS, CH, COLS), BF16),
            jax.ShapeDtypeStruct((3, 3, 3, CH, CH), F32),
            jax.ShapeDtypeStruct((1, CH), F32),
            jax.ShapeDtypeStruct((1, CH), F32),
        ),
        in_specs=[any_space] * 3,
        out_specs=(any_space, any_space, in_vmem, in_vmem),
        scratch_shapes=[
            vmem((FRAMES, ROWS, CH, COLS), BF16),
            vmem((FLAT, 128), BF16),
            vmem((8, 128), F32),
            vmem((3, 3, 3, CH, CH), F32),
            pltpu.SemaphoreType.DMA((9,)),
        ],
        compiler_params=pltpu.CompilerParams(vmem_limit_bytes=60 * 1024 * 1024),
    )(out, final, small)
    return (out, grad.transpose(0, 1, 3, 2, 4), gain.reshape(CH), shift.reshape(CH))


def solution(mesh):
    sizes = (mesh.shape["block"], mesh.shape["tile"] // 4)
    placed = (P("block", "tile", None, None), P("block", "tile", None, None), P(), P(), P())
    return jax.shard_map(
        functools.partial(shards, sizes),
        mesh=mesh,
        in_specs=placed,
        out_specs=(P("block", "tile", None, None), P(), P(), P()),
        check_vma=False,
    )
```

```python
import functools

import jax
import jax.numpy as jnp
from jax import lax
from jax.experimental import pallas as pl
from jax.experimental.pallas import tpu as pltpu
from jax.sharding import PartitionSpec as P

MESH = pl.DeviceIdType.MESH
GROUPS = 32
LOSS_SCALE = 1024.0
EPSILON = 1e-06
F32 = jnp.float32
BF16 = jnp.bfloat16

FRAMES, ROWS, CH, COLS = 4, 2, 96, 256
TAPS = 9 * CH
KEPT = 240
MOVED = TAPS - KEPT
SEG = 48
FLAT = 2048
HALF = FLAT // 2


def group_sum(values, lane):
    place = lax.rem(lane, 3)
    one_up = pltpu.roll(values, 127, 1)
    two_up = pltpu.roll(values, 126, 1)
    one_down = pltpu.roll(values, 1, 1)
    two_down = pltpu.roll(values, 2, 1)
    first = jnp.where(place == 0, one_up, one_down)
    second = jnp.where(place == 2, two_down, jnp.where(place == 0, two_up, one_up))
    return values + first + second


def body(
    sizes,
    x_hbm, g_hbm, w_hbm, gain_hbm, shift_hbm,
    out_hbm, fin_hbm, small_hbm,
    gain_ref, shift_ref, outv, small_ref, xv, gp, wv, wst, factor, normed, acts, acc, pre,
    packed, core_send, core_got, plane_send, plane_got, z_send, z_got,
    final, plane_fin, tmat, st_send, quad_got, st_mid, col_got, blk_send, blk_got,
    loc_sem, ssem, rsem,
):
    nb, nz = sizes
    ny = nb // 2
    plane = 2 * nb
    share = HALF // plane
    b = lax.axis_index("block")
    t = lax.axis_index("tile")
    nt = 4 * nz
    z = t // 4
    xh = lax.rem(t, 4) // 2
    c = lax.rem(t, 2)
    xl, y = b // ny, lax.rem(b, ny)
    flip_c = t + 1 - 2 * c
    flip_x = t + 2 - 4 * xh
    flip_cx = flip_c + 2 - 4 * xh
    across = lax.rem(t + nt - 1 + 2 * c, nt)
    b_up = lax.rem(b + 1, nb)
    b_down = lax.rem(b + nb - 1, nb)
    me = xh * nb + b

    counter = [0]

    def remote(src, dst, device):
        i = counter[0]
        counter[0] += 1
        return pltpu.make_async_remote_copy(
            src_ref=src, dst_ref=dst, send_sem=ssem.at[i], recv_sem=rsem.at[i],
            device_id=device, device_id_type=MESH,
        )

    def plane_at(dx, dy):
        x = lax.rem(2 * xh + xl + dx, 4)
        yy = lax.rem(y + dy, ny)
        hi, lo = x // 2, lax.rem(x, 2)
        block = lo * ny + yy
        return hi * nb + block, (block, t + 2 * (hi - xh))

    steps = [(dx, dy) for dx in range(4) for dy in range(ny) if (dx, dy) != (0, 0)]
    steps.sort(key=lambda d: -min(d[0], 4 - d[0]) - min(d[1], ny - d[1]))
    to_plane = [plane_at(dx, dy) for dx, dy in steps]
    from_plane = [plane_at((4 - dx) % 4, (ny - dy) % ny) for dx, dy in steps]

    barrier = pltpu.get_barrier_semaphore()
    far_first = sorted(range(1, nz), key=lambda d: -min(d, nz - d))
    column = [(b, lax.rem(t + 4 * d, nt)) for d in far_first]
    hops = [(min(dx, 4 - dx) + min(dy, ny - dy), place[1]) for (dx, dy), place in zip(steps, to_plane)]
    hops += [(min(d, nz - d), device) for d, device in zip(far_first, column)]
    hops.sort(key=lambda pair: -pair[0])
    friends = [device for _, device in hops]
    friends += [(b, across), (b_up, across), (b_down, across), (b, flip_c), (b, flip_cx)]
    for device in friends:
        pl.semaphore_signal(barrier, inc=1, device_id=device, device_id_type=MESH)

    load_x = pltpu.make_async_copy(x_hbm, xv, loc_sem.at[0])
    load_g = pltpu.make_async_copy(g_hbm, gp.at[pl.ds(0, FRAMES), pl.ds(1, ROWS)], loc_sem.at[1])
    load_w = pltpu.make_async_copy(w_hbm, wv, loc_sem.at[2])
    load_gain = pltpu.make_async_copy(gain_hbm, gain_ref, loc_sem.at[3])
    load_shift = pltpu.make_async_copy(shift_hbm, shift_ref, loc_sem.at[4])
    load_x.start()
    load_g.start()
    load_gain.start()
    load_shift.start()
    load_w.start()

    lane = lax.broadcasted_iota(jnp.int32, (CH, 128), 1)
    lane8 = lax.broadcasted_iota(jnp.int32, (8, 128), 1)
    row8 = lax.broadcasted_iota(jnp.int32, (8, 128), 0)
    col = lax.broadcasted_iota(jnp.int32, (CH, COLS), 1)
    tmat[...] = jnp.zeros((128, 128), F32)

    def channel_tile(columns):
        table = jnp.zeros((CH, 128), F32)
        for k, value in enumerate(columns):
            table = jnp.where(lane == k, value, table)
        tmat[0:CH, :] = table
        return tmat[...].T[0:8, :]

    def channel_columns(tile):
        tmat[0:8, :] = tile
        return tmat[...].T[0:CH, :]

    def halved(value):
        return value[:, 0:128] + value[:, 128:256]

    load_x.wait()
    firsts, seconds = [], []
    for f in range(FRAMES):
        one, two = jnp.zeros((CH, 128), F32), jnp.zeros((CH, 128), F32)
        for r in range(ROWS):
            value = xv[f, r].astype(F32)
            one = one + halved(value)
            two = two + halved(value * value)
        firsts.append(jnp.sum(one, axis=1, keepdims=True))
        seconds.append(jnp.sum(two, axis=1, keepdims=True))
    st_send[0] = channel_tile(firsts + seconds)

    pl.semaphore_wait(barrier, len(friends))

    has_across = jnp.where(c == 0, t > 0, t < nt - 1)
    has_down, has_up = b > 0, b < nb - 1
    four, two, late = pl.ds(0, FRAMES), pl.ds(0, 2), pl.ds(FRAMES, 2)
    core_edge, far_edge = 3 - 3 * c, 3 * c
    rows_far = remote(g_hbm.at[four, c], gp.at[four, 3 - 3 * c], (b, across))
    rows_core = remote(g_hbm.at[four, 1 - c], gp.at[four, 3 * c], (b, flip_c))
    next_two = remote(g_hbm.at[two], gp.at[late, pl.ds(1, ROWS)], (b_down, t))
    corner_far = remote(g_hbm.at[two, c], gp.at[late, 3 - 3 * c], (b_down, across))
    corner_core = remote(gp.at[late, 2 - c], gp.at[late, 3 * c], (b, flip_c))

    def all_sum(tile, at):
        quad = 2 * xh + c
        copies = []
        for k, other in enumerate((flip_c, flip_x, flip_cx)):
            slot = lax.rem(other, 4)
            copies.append((
                remote(st_send.at[at], quad_got.at[at, quad], (b, other)),
                quad_got.at[at, slot],
            ))
        for copy, _ in copies:
            copy.start()
        quad_got[at, quad] = tile
        return copies

    def quad_sum(copies, at):
        for copy, _ in copies:
            copy.wait_recv()
        total = quad_got[at, 0]
        for k in range(1, 4):
            total = total + quad_got[at, k]
        st_mid[at] = total
        out = []
        for device in column:
            out.append(remote(st_mid.at[at], col_got.at[at, z], device))
        for copy in out:
            copy.start()
        col_got[at, z] = total
        return out

    def col_sum(copies, at):
        for copy in copies:
            copy.wait_recv()
        total = col_got[at, 0]
        for k in range(1, nz):
            total = total + col_got[at, k]
        return total

    waiting = []
    stat_copies = all_sum(st_send[0], 0)
    pl.when(has_down)(next_two.start)
    pl.when(has_across)(rows_far.start)
    rows_core.start()

    @pl.when(jnp.logical_not(has_across))
    def _():
        gp[:, far_edge] = jnp.zeros((FRAMES + 2, CH, COLS), BF16)

    @pl.when(jnp.logical_not(has_up))
    def _():
        gp[late] = jnp.zeros((2, 4, CH, COLS), BF16)

    acc[...] = jnp.zeros_like(acc)
    acts[...] = jnp.zeros_like(acts)
    stat_copies_z = quad_sum(stat_copies, 0)
    pl.when(jnp.logical_and(has_down, has_across))(corner_far.start)
    waiting += [copy for copy, _ in stat_copies] + stat_copies_z

    load_w.wait()
    for r in range(3):
        slab = jnp.concatenate(
            [wv[2 - p, 2 - q, r] for p in range(3) for q in range(3)], axis=0
        )
        wst[r * CH : (r + 1) * CH, :] = slab.astype(F32).T.astype(BF16)

    number = float(nt * ROWS * COLS * (CH // GROUPS))
    sums = group_sum(col_sum(stat_copies_z, 0), lane8) / number
    center_rows = sums
    square_rows = pltpu.roll(sums, 4, 0)
    spread_rows = lax.rsqrt(square_rows - center_rows * center_rows + EPSILON)
    both = jnp.where(row8 < 4, center_rows, pltpu.roll(spread_rows, 4, 0))
    tmat[...] = jnp.zeros((128, 128), F32)
    stats = channel_columns(both)
    load_gain.wait()
    load_shift.wait()
    tmat[0:1, 0:CH] = gain_ref[...]
    tmat[1:2, 0:CH] = shift_ref[...]
    gain_rows = jnp.broadcast_to(tmat[0:1, :], (8, 128))
    vectors = tmat[...].T[0:CH, :]
    gain, shift = vectors[:, 0:1], vectors[:, 1:2]

    def kernel_terms(late_frames, edge_rows, frames=range(FRAMES)):
        for f in frames:
            lo, hi = (max(f, FRAMES), f + 3) if late_frames else (f, min(f + 3, FRAMES))
            if lo >= hi:
                continue
            for r in range(ROWS):
                if edge_rows:
                    top, rows = 3 * r, 1
                else:
                    top, rows = 1, 2
                window = gp[lo:hi, top : top + rows].reshape((hi - lo) * rows * CH, COLS)
                product = lax.dot_general(
                    window, acts[f * ROWS + r], (((1,), (1,)), ((), ())),
                    preferred_element_type=F32,
                )
                height = rows * CH
                for k in range(hi - lo):
                    row = (3 * (lo + k - f) + top - r) * CH
                    acc[row : row + height] += product[k * height : (k + 1) * height]

    @pl.when(has_up)
    def _():
        next_two.wait_recv()
        corner_core.start()

    load_g.wait()
    for f in range(FRAMES):
        center, spread = stats[:, f : f + 1], stats[:, 4 + f : 5 + f]
        for r in range(ROWS):
            n = f * ROWS + r
            scaled = (xv[f, r].astype(F32) - center) * spread
            shaped = scaled * gain + shift
            logistic = 1.0 / (1.0 + jnp.exp(-shaped))
            active = shaped * logistic
            normed[n] = scaled
            factor[n] = logistic * (1.0 + shaped * (1.0 - logistic))
            before = jnp.where(col == 0, 0.0, pltpu.roll(active, 1, 1))
            after = jnp.where(col == COLS - 1, 0.0, pltpu.roll(active, COLS - 1, 1))
            acts[n, 0:CH] = before.astype(BF16)
            acts[n, 128 : 128 + CH] = active.astype(BF16)
            acts[n, 256 : 256 + CH] = after.astype(BF16)
        kernel_terms(False, False, (f,))

    kernel_terms(True, False)
    rows_core.wait_recv()
    pl.when(has_across)(rows_far.wait_recv)
    kernel_terms(False, True)
    pl.when(has_up)(corner_core.wait_recv)
    pl.when(jnp.logical_and(has_up, has_across))(corner_far.wait_recv)
    kernel_terms(True, True)

    lanes = lax.broadcasted_iota(jnp.int32, (SEG, 128), 1)
    for row in range(0, 2 * TAPS + KEPT, SEG):
        slab, first = row // TAPS, row % TAPS
        value = acc[first : first + SEG, 128 * slab : 128 * slab + 128]
        k, source = row // MOVED, KEPT + row % MOVED
        if k < 3:
            extra = pltpu.roll(acc[source : source + SEG, 256:384], CH - 32 * k, 1)
            value = jnp.where(lanes < CH, value, extra)
        packed[row : row + SEG] = value
    packed[2 * TAPS + KEPT : FLAT] = jnp.zeros((FLAT - 2 * TAPS - KEPT, 128), F32)

    mine = pl.multiple_of(c * HALF, HALF)
    theirs = pl.multiple_of((1 - c) * HALF, HALF)
    core_send[...] = packed[pl.ds(theirs, HALF)].astype(BF16)
    core_copy = remote(core_send, core_got, (b, flip_c))
    core_copy.start()

    def act_grad(n):
        f, r = n // ROWS, lax.rem(n, ROWS)
        window = gp[pl.ds(f, 3), pl.ds(r, 3)].reshape(TAPS, COLS)
        product = jnp.dot(wst[...], window, preferred_element_type=F32)
        after = pltpu.roll(product[0:CH], COLS - 1, 1)
        before = pltpu.roll(product[2 * CH : 3 * CH], 1, 1)
        after = jnp.where(col == COLS - 1, 0.0, after)
        before = jnp.where(col == 0, 0.0, before)
        pre[n] = (after + product[CH : 2 * CH] + before) * factor[n]

    pl.loop(0, 4)(act_grad)
    core_copy.wait_recv()
    chip = packed[pl.ds(mine, HALF)] + core_got[...].astype(F32)
    packed[pl.ds(mine, HALF)] = chip
    plane_send[...] = chip.astype(BF16)
    plane_copies = []
    for k, (place, device) in enumerate(to_plane):
        rows = pl.ds(pl.multiple_of(place * share, share), share)
        plane_copies.append(remote(plane_send.at[rows], plane_got.at[k], device))
    for copy in plane_copies:
        copy.start()

    pl.loop(4, FRAMES * ROWS)(act_grad)

    firsts, seconds = [], []
    for f in range(FRAMES):
        one, two = jnp.zeros((CH, 128), F32), jnp.zeros((CH, 128), F32)
        for r in range(ROWS):
            n = f * ROWS + r
            value = pre[n]
            one = one + halved(value)
            two = two + halved(value * normed[n])
        firsts.append(jnp.sum(one, axis=1, keepdims=True))
        seconds.append(jnp.sum(two, axis=1, keepdims=True))
    tmat[...] = jnp.zeros((128, 128), F32)
    st_send[1] = channel_tile(firsts + seconds)
    stat_copies = all_sum(st_send[1], 1)

    for copy in plane_copies:
        copy.wait_recv()
    part = packed[pl.ds(pl.multiple_of(mine + me * share, share), share)]
    for k in range(plane - 1):
        part = part + plane_got[k].astype(F32)
    z_send[...] = part.astype(BF16)
    z_got[z] = part.astype(BF16)
    z_copies = [remote(z_send, z_got.at[z], device) for device in column]
    for copy in z_copies:
        copy.start()

    stat_copies_z = quad_sum(stat_copies, 1)
    waiting += [copy for copy, _ in stat_copies] + stat_copies_z

    for copy in z_copies:
        copy.wait_recv()
    part = z_got[0].astype(F32)
    for k in range(1, nz):
        part = part + z_got[k].astype(F32)
    plane_fin[...] = (part * (1.0 / LOSS_SCALE)).astype(BF16)
    own_rows = pl.ds(pl.multiple_of(mine + me * share, share), share)
    final[own_rows] = plane_fin[...]
    spread_copies = []
    for place, device in to_plane:
        spread_copies.append(remote(plane_fin, final.at[own_rows], device))
    for copy in spread_copies:
        copy.start()
    pass_copies = [remote(plane_fin, final.at[own_rows], (b, flip_c))]
    pass_copies[0].start()

    total = col_sum(stat_copies_z, 1)
    means = channel_columns(group_sum(total * gain_rows, lane8) / number)

    pairs = total + pltpu.roll(total, 2, 0)
    pairs = pairs + pltpu.roll(pairs, 1, 0)
    blk_send[...] = pairs
    blk_got[b] = pairs
    blk_copies = []
    for d in range(1, nb):
        block = lax.rem(b + d, nb)
        blk_copies.append(remote(blk_send, blk_got.at[b], (block, t)))
    for copy in blk_copies:
        copy.start()

    for f in range(FRAMES):
        spread = stats[:, 4 + f : 5 + f]
        m1, m2 = means[:, f : f + 1], means[:, 4 + f : 5 + f]
        for r in range(ROWS):
            n = f * ROWS + r
            value = spread * (pre[n] * gain - m1 - normed[n] * m2)
            outv[f, r] = value.astype(BF16)
    store_x = pltpu.make_async_copy(outv, out_hbm, loc_sem.at[5])
    store_x.start()

    pl.when(has_down)(next_two.wait_send)
    pl.when(has_across)(rows_far.wait_send)
    pl.when(jnp.logical_and(has_down, has_across))(corner_far.wait_send)
    pl.when(has_up)(corner_core.wait_send)
    waiting += [core_copy, rows_core] + plane_copies + z_copies
    for copy in waiting:
        copy.wait_send()

    for copy, (place, _) in reversed(list(zip(spread_copies, from_plane))):
        copy.wait_recv()
        rows = pl.ds(pl.multiple_of(mine + place * share, share), share)
        pass_copies.append(remote(final.at[rows], final.at[rows], (b, flip_c)))
        pass_copies[-1].start()
    store_mine = pltpu.make_async_copy(
        final.at[pl.ds(mine, HALF)], fin_hbm.at[pl.ds(mine, HALF)], loc_sem.at[7]
    )
    store_mine.start()
    for copy in blk_copies:
        copy.wait_recv()
    total = blk_got[0]
    for k in range(1, nb):
        total = total + blk_got[k]
    small_ref[...] = total / LOSS_SCALE
    store_small = pltpu.make_async_copy(small_ref, small_hbm, loc_sem.at[6])
    store_small.start()

    for copy in pass_copies:
        copy.wait_recv()

    store_theirs = pltpu.make_async_copy(
        final.at[pl.ds(theirs, HALF)], fin_hbm.at[pl.ds(theirs, HALF)], loc_sem.at[8]
    )
    store_theirs.start()

    for copy in blk_copies + spread_copies + pass_copies:
        copy.wait_send()
    store_x.wait()
    store_small.wait()
    store_mine.wait()
    store_theirs.wait()


def unpack_body(
    out_in, fin_in, small_in, out_hbm, kg_hbm, gain_hbm, shift_hbm,
    out_ref, fin_ref, small_ref, vectors, kg, sems,
):
    bounds = (0, TAPS, 2 * TAPS, FLAT)
    loads = []
    for k in range(3):
        rows = pl.ds(bounds[k], bounds[k + 1] - bounds[k])
        loads.append(pltpu.make_async_copy(fin_in.at[rows], fin_ref.at[rows], sems.at[k]))
        loads[k].start()
    load_out = pltpu.make_async_copy(out_in, out_ref, sems.at[3])
    load_out.start()
    load_small = pltpu.make_async_copy(small_in, small_ref, sems.at[4])
    load_small.start()
    lanes = lax.broadcasted_iota(jnp.int32, (16, 128), 1)
    stores = []
    for r in range(3):
        loads[r].wait()
        for p in range(3):
            for q in range(3):
                tap = ((2 - p) * 3 + 2 - q) * CH
                if r < 2:
                    slab = fin_ref[r * TAPS + tap : r * TAPS + tap + CH].astype(F32)
                    kg[p, q, r] = slab[:, 0:CH]
                    continue
                for first in range(tap, tap + CH, 16):
                    if first < KEPT:
                        slab = fin_ref[2 * TAPS + first : 2 * TAPS + first + 16].astype(F32)
                    else:
                        slab = None
                        for k in range(3):
                            row = MOVED * k + first - KEPT
                            piece = fin_ref[row : row + 16].astype(F32)
                            piece = pltpu.roll(piece, 32 + 32 * k, 1)
                            slab = piece if k == 0 else jnp.where(lanes // 32 == k, piece, slab)
                    kg[p, q, 2, first - tap : first - tap + 16] = slab[:, 0:CH]
        store = pltpu.make_async_copy(kg.at[:, :, r], kg_hbm.at[:, :, r], sems.at[5 + r])
        store.start()
        stores.append(store)
        if r == 0:
            load_out.wait()
            load_small.wait()
            vectors[0, 0:1] = small_ref[7:8, 0:CH]
            vectors[1, 0:1] = small_ref[3:4, 0:CH]
            others = [
                pltpu.make_async_copy(out_ref, out_hbm, sems.at[8]),
                pltpu.make_async_copy(vectors.at[0, pl.ds(0, 1)], gain_hbm, sems.at[9]),
                pltpu.make_async_copy(vectors.at[1, pl.ds(0, 1)], shift_hbm, sems.at[10]),
            ]
            for copy in others:
                copy.start()
            stores += others
    for copy in stores:
        copy.wait()


def shards(sizes, inputs, out_grads, kernel, norm_gain, norm_shift):
    nb, nz = sizes
    plane = 2 * nb
    share = HALF // plane
    copies = 5 + 2 * (3 + nz - 1) + 1 + 2 * (plane - 1) + (nz - 1) + nb - 1 + plane
    vmem = pltpu.VMEM
    any_space = pl.BlockSpec(memory_space=pl.ANY)
    cells = FRAMES * ROWS
    out, final, small = pl.pallas_call(
        functools.partial(body, sizes),
        out_shape=(
            jax.ShapeDtypeStruct((FRAMES, ROWS, CH, COLS), BF16),
            jax.ShapeDtypeStruct((FLAT, 128), BF16),
            jax.ShapeDtypeStruct((8, 128), F32),
        ),
        in_specs=[any_space] * 5,
        out_specs=(any_space,) * 3,
        scratch_shapes=[
            vmem((1, CH), F32),
            vmem((1, CH), F32),
            vmem((FRAMES, ROWS, CH, COLS), BF16),
            vmem((8, 128), F32),
            vmem((FRAMES, ROWS, CH, COLS), BF16),
            vmem((FRAMES + 2, ROWS + 2, CH, COLS), BF16),
            vmem((3, 3, 3, CH, CH), BF16),
            vmem((3 * CH, TAPS), BF16),
            vmem((cells, CH, COLS), F32),
            vmem((cells, CH, COLS), F32),
            vmem((cells, 3 * 128, COLS), BF16),
            vmem((TAPS, 3 * 128), F32),
            vmem((cells, CH, COLS), F32),
            vmem((FLAT, 128), F32),
            vmem((HALF, 128), BF16),
            vmem((HALF, 128), BF16),
            vmem((HALF, 128), BF16),
            vmem((plane - 1, share, 128), BF16),
            vmem((share, 128), BF16),
            vmem((nz, share, 128), BF16),
            vmem((FLAT, 128), BF16),
            vmem((share, 128), BF16),
            vmem((128, 128), F32),
            vmem((2, 8, 128), F32),
            vmem((2, 4, 8, 128), F32),
            vmem((2, 8, 128), F32),
            vmem((2, nz, 8, 128), F32),
            vmem((8, 128), F32),
            vmem((nb, 8, 128), F32),
            pltpu.SemaphoreType.DMA((9,)),
            pltpu.SemaphoreType.DMA((copies,)),
            pltpu.SemaphoreType.DMA((copies,)),
        ],
        compiler_params=pltpu.CompilerParams(
            collective_id=0, has_side_effects=True, vmem_limit_bytes=60 * 1024 * 1024
        ),
    )(
        inputs, out_grads, kernel.transpose(0, 1, 3, 2, 4),
        norm_gain.reshape(1, CH), norm_shift.reshape(1, CH),
    )
    out, grad, gain, shift = pl.pallas_call(
        unpack_body,
        out_shape=(
            jax.ShapeDtypeStruct((FRAMES, ROWS, CH, COLS), BF16),
            jax.ShapeDtypeStruct((3, 3, 3, CH, CH), F32),
            jax.ShapeDtypeStruct((1, CH), F32),
            jax.ShapeDtypeStruct((1, CH), F32),
        ),
        in_specs=[any_space] * 3,
        out_specs=(any_space,) * 4,
        scratch_shapes=[
            vmem((FRAMES, ROWS, CH, COLS), BF16),
            vmem((FLAT, 128), BF16),
            vmem((8, 128), F32),
            vmem((2, 8, CH), F32),
            vmem((3, 3, 3, CH, CH), F32),
            pltpu.SemaphoreType.DMA((11,)),
        ],
        compiler_params=pltpu.CompilerParams(vmem_limit_bytes=60 * 1024 * 1024),
    )(out, final, small)
    return (out, grad.transpose(0, 1, 3, 2, 4), gain.reshape(CH), shift.reshape(CH))


def solution(mesh):
    sizes = (mesh.shape["block"], mesh.shape["tile"] // 4)
    placed = (P("block", "tile", None, None), P("block", "tile", None, None), P(), P(), P())
    return jax.shard_map(
        functools.partial(shards, sizes),
        mesh=mesh,
        in_specs=placed,
        out_specs=(P("block", "tile", None, None), P(), P(), P()),
        check_vma=False,
    )
```

```python
import functools

import jax
import jax.numpy as jnp
from jax import lax
from jax.experimental import pallas as pl
from jax.experimental.pallas import tpu as pltpu
from jax.sharding import PartitionSpec as P

MESH = pl.DeviceIdType.MESH
GROUPS = 32
LOSS_SCALE = 1024.0
EPSILON = 1e-06
F32 = jnp.float32
BF16 = jnp.bfloat16

FRAMES, ROWS, CH, COLS = 4, 2, 96, 256
TAPS = 9 * CH
KEPT = 240
MOVED = TAPS - KEPT
SEG = 48
FLAT = 2048
HALF = FLAT // 2


def group_sum(values, lane):
    place = lax.rem(lane, 3)
    one_up = pltpu.roll(values, 127, 1)
    two_up = pltpu.roll(values, 126, 1)
    one_down = pltpu.roll(values, 1, 1)
    two_down = pltpu.roll(values, 2, 1)
    first = jnp.where(place == 0, one_up, one_down)
    second = jnp.where(place == 2, two_down, jnp.where(place == 0, two_up, one_up))
    return values + first + second


def body(
    sizes,
    x_hbm, g_hbm, w_hbm, gain_hbm, shift_hbm,
    out_hbm, fin_hbm, small_hbm,
    gain_ref, shift_ref, outv, small_ref, xv, gp, wv, wst, factor, normed, acts, acc, pre,
    packed, core_send, core_got, plane_send, plane_got, z_send, z_got,
    final, plane_fin, tmat, st_send, quad_got, st_mid, col_got, blk_send, blk_got,
    loc_sem, ssem, rsem,
):
    nb, nz = sizes
    ny = nb // 2
    plane = 2 * nb
    share = HALF // plane
    b = lax.axis_index("block")
    t = lax.axis_index("tile")
    nt = 4 * nz
    z = t // 4
    xh = lax.rem(t, 4) // 2
    c = lax.rem(t, 2)
    xl, y = b // ny, lax.rem(b, ny)
    flip_c = t + 1 - 2 * c
    flip_x = t + 2 - 4 * xh
    flip_cx = flip_c + 2 - 4 * xh
    across = lax.rem(t + nt - 1 + 2 * c, nt)
    b_up = lax.rem(b + 1, nb)
    b_down = lax.rem(b + nb - 1, nb)
    me = xh * nb + b

    counter = [0]

    def remote(src, dst, device):
        i = counter[0]
        counter[0] += 1
        return pltpu.make_async_remote_copy(
            src_ref=src, dst_ref=dst, send_sem=ssem.at[i], recv_sem=rsem.at[i],
            device_id=device, device_id_type=MESH,
        )

    def plane_at(dx, dy):
        x = lax.rem(2 * xh + xl + dx, 4)
        yy = lax.rem(y + dy, ny)
        hi, lo = x // 2, lax.rem(x, 2)
        block = lo * ny + yy
        return hi * nb + block, (block, t + 2 * (hi - xh))

    steps = [(dx, dy) for dx in range(4) for dy in range(ny) if (dx, dy) != (0, 0)]
    steps.sort(key=lambda d: -min(d[0], 4 - d[0]) - min(d[1], ny - d[1]))
    to_plane = [plane_at(dx, dy) for dx, dy in steps]
    from_plane = [plane_at((4 - dx) % 4, (ny - dy) % ny) for dx, dy in steps]

    barrier = pltpu.get_barrier_semaphore()
    far_first = sorted(range(1, nz), key=lambda d: -min(d, nz - d))
    column = [(b, lax.rem(t + 4 * d, nt)) for d in far_first]
    hops = [(min(dx, 4 - dx) + min(dy, ny - dy), place[1]) for (dx, dy), place in zip(steps, to_plane)]
    hops += [(min(d, nz - d), device) for d, device in zip(far_first, column)]
    hops.sort(key=lambda pair: -pair[0])
    friends = [device for _, device in hops]
    friends += [(b, across), (b_up, across), (b_down, across), (b, flip_c), (b, flip_cx)]
    for device in friends:
        pl.semaphore_signal(barrier, inc=1, device_id=device, device_id_type=MESH)

    load_x = pltpu.make_async_copy(x_hbm, xv, loc_sem.at[0])
    load_g = pltpu.make_async_copy(g_hbm, gp.at[pl.ds(0, FRAMES), pl.ds(1, ROWS)], loc_sem.at[1])
    load_w = pltpu.make_async_copy(w_hbm, wv, loc_sem.at[2])
    load_gain = pltpu.make_async_copy(gain_hbm, gain_ref, loc_sem.at[3])
    load_shift = pltpu.make_async_copy(shift_hbm, shift_ref, loc_sem.at[4])
    load_x.start()
    load_g.start()
    load_gain.start()
    load_shift.start()
    load_w.start()

    lane = lax.broadcasted_iota(jnp.int32, (CH, 128), 1)
    lane8 = lax.broadcasted_iota(jnp.int32, (8, 128), 1)
    row8 = lax.broadcasted_iota(jnp.int32, (8, 128), 0)
    col = lax.broadcasted_iota(jnp.int32, (CH, COLS), 1)
    tmat[...] = jnp.zeros((128, 128), F32)

    def channel_tile(columns):
        table = jnp.zeros((CH, 128), F32)
        for k, value in enumerate(columns):
            table = jnp.where(lane == k, value, table)
        tmat[0:CH, :] = table
        return tmat[...].T[0:8, :]

    def channel_columns(tile):
        tmat[0:8, :] = tile
        return tmat[...].T[0:CH, :]

    def halved(value):
        return value[:, 0:128] + value[:, 128:256]

    load_x.wait()
    firsts, seconds = [], []
    for f in range(FRAMES):
        one, two = jnp.zeros((CH, 128), F32), jnp.zeros((CH, 128), F32)
        for r in range(ROWS):
            value = xv[f, r].astype(F32)
            one = one + halved(value)
            two = two + halved(value * value)
        firsts.append(jnp.sum(one, axis=1, keepdims=True))
        seconds.append(jnp.sum(two, axis=1, keepdims=True))
    st_send[0] = channel_tile(firsts + seconds)

    pl.semaphore_wait(barrier, len(friends))

    has_across = jnp.where(c == 0, t > 0, t < nt - 1)
    has_down, has_up = b > 0, b < nb - 1
    four, two, late = pl.ds(0, FRAMES), pl.ds(0, 2), pl.ds(FRAMES, 2)
    core_edge, far_edge = 3 - 3 * c, 3 * c
    rows_far = remote(g_hbm.at[four, c], gp.at[four, 3 - 3 * c], (b, across))
    rows_core = remote(g_hbm.at[four, 1 - c], gp.at[four, 3 * c], (b, flip_c))
    next_two = remote(g_hbm.at[two], gp.at[late, pl.ds(1, ROWS)], (b_down, t))
    corner_far = remote(g_hbm.at[two, c], gp.at[late, 3 - 3 * c], (b_down, across))
    corner_core = remote(gp.at[late, 2 - c], gp.at[late, 3 * c], (b, flip_c))

    def all_sum(tile, at):
        quad = 2 * xh + c
        copies = []
        for k, other in enumerate((flip_c, flip_x, flip_cx)):
            slot = lax.rem(other, 4)
            copies.append((
                remote(st_send.at[at], quad_got.at[at, quad], (b, other)),
                quad_got.at[at, slot],
            ))
        for copy, _ in copies:
            copy.start()
        quad_got[at, quad] = tile
        return copies

    def quad_sum(copies, at):
        for copy, _ in copies:
            copy.wait_recv()
        total = quad_got[at, 0]
        for k in range(1, 4):
            total = total + quad_got[at, k]
        st_mid[at] = total
        out = []
        for device in column:
            out.append(remote(st_mid.at[at], col_got.at[at, z], device))
        for copy in out:
            copy.start()
        col_got[at, z] = total
        return out

    def col_sum(copies, at):
        for copy in copies:
            copy.wait_recv()
        total = col_got[at, 0]
        for k in range(1, nz):
            total = total + col_got[at, k]
        return total

    waiting = []
    stat_copies = all_sum(st_send[0], 0)
    pl.when(has_down)(next_two.start)
    pl.when(has_across)(rows_far.start)
    rows_core.start()

    @pl.when(jnp.logical_not(has_across))
    def _():
        gp[:, far_edge] = jnp.zeros((FRAMES + 2, CH, COLS), BF16)

    @pl.when(jnp.logical_not(has_up))
    def _():
        gp[late] = jnp.zeros((2, 4, CH, COLS), BF16)

    acc[...] = jnp.zeros_like(acc)
    acts[...] = jnp.zeros_like(acts)
    stat_copies_z = quad_sum(stat_copies, 0)
    pl.when(jnp.logical_and(has_down, has_across))(corner_far.start)
    waiting += [copy for copy, _ in stat_copies] + stat_copies_z

    load_w.wait()
    for r in range(3):
        slab = jnp.concatenate(
            [wv[2 - p, 2 - q, r] for p in range(3) for q in range(3)], axis=0
        )
        wst[r * CH : (r + 1) * CH, :] = slab.astype(F32).T.astype(BF16)

    tmat[...] = jnp.zeros((128, 128), F32)
    load_gain.wait()
    load_shift.wait()
    tmat[0:1, 0:CH] = gain_ref[...]
    tmat[1:2, 0:CH] = shift_ref[...]
    gain_rows = jnp.broadcast_to(tmat[0:1, :], (8, 128))
    vectors = tmat[...].T[0:CH, :]
    gain, shift = vectors[:, 0:1], vectors[:, 1:2]
    number = float(nt * ROWS * COLS * (CH // GROUPS))
    sums = group_sum(col_sum(stat_copies_z, 0), lane8) / number
    center_rows = sums
    square_rows = pltpu.roll(sums, 4, 0)
    spread_rows = lax.rsqrt(square_rows - center_rows * center_rows + EPSILON)
    both = jnp.where(row8 < 4, center_rows, pltpu.roll(spread_rows, 4, 0))
    stats = channel_columns(both)

    def kernel_terms(late_frames, edge_rows, frames=range(FRAMES)):
        for f in frames:
            lo, hi = (max(f, FRAMES), f + 3) if late_frames else (f, min(f + 3, FRAMES))
            if lo >= hi:
                continue
            for top, r_lo, r_hi in ((0, 0, 1), (3, 1, 2)) if edge_rows else ((1, 0, 2),):
                rows = r_hi - r_lo
                height = rows * CH
                window = gp[lo:hi, top : top + rows].reshape((hi - lo) * height, COLS)
                both = acts[f * ROWS + r_lo : f * ROWS + r_hi].reshape(rows * 384, COLS)
                product = lax.dot_general(
                    window, both, (((1,), (1,)), ((), ())), preferred_element_type=F32
                )
                for r in range(r_lo, r_hi):
                    term = product[:, (r - r_lo) * 384 : (r - r_lo + 1) * 384]
                    for k in range(hi - lo):
                        row = (3 * (lo + k - f) + top - r) * CH
                        acc[row : row + height] += term[k * height : (k + 1) * height]

    @pl.when(has_up)
    def _():
        next_two.wait_recv()
        corner_core.start()

    load_g.wait()
    for f in range(FRAMES):
        center, spread = stats[:, f : f + 1], stats[:, 4 + f : 5 + f]
        for r in range(ROWS):
            n = f * ROWS + r
            scaled = (xv[f, r].astype(F32) - center) * spread
            shaped = scaled * gain + shift
            logistic = 1.0 / (1.0 + jnp.exp(-shaped))
            active = shaped * logistic
            normed[n] = scaled
            factor[n] = logistic * (1.0 + shaped * (1.0 - logistic))
            before = jnp.where(col == 0, 0.0, pltpu.roll(active, 1, 1))
            after = jnp.where(col == COLS - 1, 0.0, pltpu.roll(active, COLS - 1, 1))
            acts[n, 0:CH] = before.astype(BF16)
            acts[n, 128 : 128 + CH] = active.astype(BF16)
            acts[n, 256 : 256 + CH] = after.astype(BF16)
        kernel_terms(False, False, (f,))

    kernel_terms(True, False)
    rows_core.wait_recv()
    pl.when(has_across)(rows_far.wait_recv)
    kernel_terms(False, True)
    pl.when(has_up)(corner_core.wait_recv)
    pl.when(jnp.logical_and(has_up, has_across))(corner_far.wait_recv)
    kernel_terms(True, True)

    lanes = lax.broadcasted_iota(jnp.int32, (SEG, 128), 1)
    for row in range(0, 2 * TAPS + KEPT, SEG):
        slab, first = row // TAPS, row % TAPS
        value = acc[first : first + SEG, 128 * slab : 128 * slab + 128]
        k, source = row // MOVED, KEPT + row % MOVED
        if k < 3:
            extra = pltpu.roll(acc[source : source + SEG, 256:384], CH - 32 * k, 1)
            value = jnp.where(lanes < CH, value, extra)
        packed[row : row + SEG] = value
    packed[2 * TAPS + KEPT : FLAT] = jnp.zeros((FLAT - 2 * TAPS - KEPT, 128), F32)

    mine = pl.multiple_of(c * HALF, HALF)
    theirs = pl.multiple_of((1 - c) * HALF, HALF)
    core_send[...] = packed[pl.ds(theirs, HALF)].astype(BF16)
    core_copy = remote(core_send, core_got, (b, flip_c))
    core_copy.start()

    def act_grad(n):
        f, r = n // ROWS, n % ROWS
        window = gp[pl.ds(f, 3), pl.ds(r, 3)].reshape(TAPS, COLS)
        product = jnp.dot(wst[...], window, preferred_element_type=F32)
        after = pltpu.roll(product[0:CH], COLS - 1, 1)
        before = pltpu.roll(product[2 * CH : 3 * CH], 1, 1)
        after = jnp.where(col == COLS - 1, 0.0, after)
        before = jnp.where(col == 0, 0.0, before)
        pre[n] = (after + product[CH : 2 * CH] + before) * factor[n]

    core_copy.wait_recv()
    chip = packed[pl.ds(mine, HALF)] + core_got[...].astype(F32)
    packed[pl.ds(mine, HALF)] = chip
    plane_send[...] = chip.astype(BF16)
    plane_copies = []
    for k, (place, device) in enumerate(to_plane):
        rows = pl.ds(pl.multiple_of(place * share, share), share)
        plane_copies.append(remote(plane_send.at[rows], plane_got.at[k], device))
    for copy in plane_copies:
        copy.start()

    for n in range(FRAMES * ROWS):
        act_grad(n)

    firsts, seconds = [], []
    for f in range(FRAMES):
        one, two = jnp.zeros((CH, 128), F32), jnp.zeros((CH, 128), F32)
        for r in range(ROWS):
            n = f * ROWS + r
            value = pre[n]
            one = one + halved(value)
            two = two + halved(value * normed[n])
        firsts.append(jnp.sum(one, axis=1, keepdims=True))
        seconds.append(jnp.sum(two, axis=1, keepdims=True))
    tmat[...] = jnp.zeros((128, 128), F32)
    st_send[1] = channel_tile(firsts + seconds)
    stat_copies = all_sum(st_send[1], 1)

    for copy in plane_copies:
        copy.wait_recv()
    part = packed[pl.ds(pl.multiple_of(mine + me * share, share), share)]
    for k in range(plane - 1):
        part = part + plane_got[k].astype(F32)
    z_send[...] = part.astype(BF16)
    z_got[z] = part.astype(BF16)
    z_copies = [remote(z_send, z_got.at[z], device) for device in column]
    for copy in z_copies:
        copy.start()

    stat_copies_z = quad_sum(stat_copies, 1)
    waiting += [copy for copy, _ in stat_copies] + stat_copies_z

    for copy in z_copies:
        copy.wait_recv()
    part = z_got[0].astype(F32)
    for k in range(1, nz):
        part = part + z_got[k].astype(F32)
    plane_fin[...] = (part * (1.0 / LOSS_SCALE)).astype(BF16)
    own_rows = pl.ds(pl.multiple_of(mine + me * share, share), share)
    final[own_rows] = plane_fin[...]
    spread_copies = []
    for place, device in to_plane:
        spread_copies.append(remote(plane_fin, final.at[own_rows], device))
    for copy in spread_copies:
        copy.start()
    pass_copies = [remote(plane_fin, final.at[own_rows], (b, flip_c))]
    pass_copies[0].start()

    total = col_sum(stat_copies_z, 1)
    means = channel_columns(group_sum(total * gain_rows, lane8) / number)

    pairs = total + pltpu.roll(total, 2, 0)
    pairs = pairs + pltpu.roll(pairs, 1, 0)
    blk_send[...] = pairs
    blk_got[b] = pairs
    blk_copies = []
    for d in range(1, nb):
        block = lax.rem(b + d, nb)
        blk_copies.append(remote(blk_send, blk_got.at[b], (block, t)))
    for copy in blk_copies:
        copy.start()

    for f in range(FRAMES):
        spread = stats[:, 4 + f : 5 + f]
        m1, m2 = means[:, f : f + 1], means[:, 4 + f : 5 + f]
        for r in range(ROWS):
            n = f * ROWS + r
            value = spread * (pre[n] * gain - m1 - normed[n] * m2)
            outv[f, r] = value.astype(BF16)
    store_x = pltpu.make_async_copy(outv, out_hbm, loc_sem.at[5])
    store_x.start()

    pl.when(has_down)(next_two.wait_send)
    pl.when(has_across)(rows_far.wait_send)
    pl.when(jnp.logical_and(has_down, has_across))(corner_far.wait_send)
    pl.when(has_up)(corner_core.wait_send)
    waiting += [core_copy, rows_core] + plane_copies + z_copies
    for copy in waiting:
        copy.wait_send()

    for copy, (place, _) in reversed(list(zip(spread_copies, from_plane))):
        copy.wait_recv()
        rows = pl.ds(pl.multiple_of(mine + place * share, share), share)
        pass_copies.append(remote(final.at[rows], final.at[rows], (b, flip_c)))
        pass_copies[-1].start()
    store_mine = pltpu.make_async_copy(
        final.at[pl.ds(mine, HALF)], fin_hbm.at[pl.ds(mine, HALF)], loc_sem.at[7]
    )
    store_mine.start()
    for copy in blk_copies:
        copy.wait_recv()
    total = blk_got[0]
    for k in range(1, nb):
        total = total + blk_got[k]
    small_ref[...] = total / LOSS_SCALE
    store_small = pltpu.make_async_copy(small_ref, small_hbm, loc_sem.at[6])
    store_small.start()

    for copy in pass_copies:
        copy.wait_recv()

    store_theirs = pltpu.make_async_copy(
        final.at[pl.ds(theirs, HALF)], fin_hbm.at[pl.ds(theirs, HALF)], loc_sem.at[8]
    )
    store_theirs.start()

    for copy in blk_copies + spread_copies + pass_copies:
        copy.wait_send()
    store_x.wait()
    store_small.wait()
    store_mine.wait()
    store_theirs.wait()


def unpack_body(
    out_in, fin_in, small_in, out_hbm, kg_hbm, gain_hbm, shift_hbm,
    out_ref, fin_ref, small_ref, vectors, kg, sems,
):
    bounds = (0, TAPS, 2 * TAPS, FLAT)
    loads = []
    for k in range(3):
        rows = pl.ds(bounds[k], bounds[k + 1] - bounds[k])
        loads.append(pltpu.make_async_copy(fin_in.at[rows], fin_ref.at[rows], sems.at[k]))
        loads[k].start()
    load_out = pltpu.make_async_copy(out_in, out_ref, sems.at[3])
    load_out.start()
    load_small = pltpu.make_async_copy(small_in, small_ref, sems.at[4])
    load_small.start()
    lanes = lax.broadcasted_iota(jnp.int32, (16, 128), 1)
    stores = []
    for r in range(3):
        loads[r].wait()
        for p in range(3):
            for q in range(3):
                tap = ((2 - p) * 3 + 2 - q) * CH
                if r < 2:
                    slab = fin_ref[r * TAPS + tap : r * TAPS + tap + CH].astype(F32)
                    kg[p, q, r] = slab[:, 0:CH]
                    continue
                for first in range(tap, tap + CH, 16):
                    if first < KEPT:
                        slab = fin_ref[2 * TAPS + first : 2 * TAPS + first + 16].astype(F32)
                    else:
                        slab = None
                        for k in range(3):
                            row = MOVED * k + first - KEPT
                            piece = fin_ref[row : row + 16].astype(F32)
                            piece = pltpu.roll(piece, 32 + 32 * k, 1)
                            slab = piece if k == 0 else jnp.where(lanes // 32 == k, piece, slab)
                    kg[p, q, 2, first - tap : first - tap + 16] = slab[:, 0:CH]
        store = pltpu.make_async_copy(kg.at[:, :, r], kg_hbm.at[:, :, r], sems.at[5 + r])
        store.start()
        stores.append(store)
        if r == 0:
            load_out.wait()
            load_small.wait()
            vectors[0, 0:1] = small_ref[7:8, 0:CH]
            vectors[1, 0:1] = small_ref[3:4, 0:CH]
            others = [
                pltpu.make_async_copy(out_ref, out_hbm, sems.at[8]),
                pltpu.make_async_copy(vectors.at[0, pl.ds(0, 1)], gain_hbm, sems.at[9]),
                pltpu.make_async_copy(vectors.at[1, pl.ds(0, 1)], shift_hbm, sems.at[10]),
            ]
            for copy in others:
                copy.start()
            stores += others
    for copy in stores:
        copy.wait()


def shards(sizes, inputs, out_grads, kernel, norm_gain, norm_shift):
    nb, nz = sizes
    plane = 2 * nb
    share = HALF // plane
    copies = 5 + 2 * (3 + nz - 1) + 1 + 2 * (plane - 1) + (nz - 1) + nb - 1 + plane
    vmem = pltpu.VMEM
    any_space = pl.BlockSpec(memory_space=pl.ANY)
    cells = FRAMES * ROWS
    out, final, small = pl.pallas_call(
        functools.partial(body, sizes),
        out_shape=(
            jax.ShapeDtypeStruct((FRAMES, ROWS, CH, COLS), BF16),
            jax.ShapeDtypeStruct((FLAT, 128), BF16),
            jax.ShapeDtypeStruct((8, 128), F32),
        ),
        in_specs=[any_space] * 5,
        out_specs=(any_space,) * 3,
        scratch_shapes=[
            vmem((1, CH), F32),
            vmem((1, CH), F32),
            vmem((FRAMES, ROWS, CH, COLS), BF16),
            vmem((8, 128), F32),
            vmem((FRAMES, ROWS, CH, COLS), BF16),
            vmem((FRAMES + 2, ROWS + 2, CH, COLS), BF16),
            vmem((3, 3, 3, CH, CH), BF16),
            vmem((3 * CH, TAPS), BF16),
            vmem((cells, CH, COLS), F32),
            vmem((cells, CH, COLS), F32),
            vmem((cells, 3 * 128, COLS), BF16),
            vmem((TAPS, 3 * 128), F32),
            vmem((cells, CH, COLS), F32),
            vmem((FLAT, 128), F32),
            vmem((HALF, 128), BF16),
            vmem((HALF, 128), BF16),
            vmem((HALF, 128), BF16),
            vmem((plane - 1, share, 128), BF16),
            vmem((share, 128), BF16),
            vmem((nz, share, 128), BF16),
            vmem((FLAT, 128), BF16),
            vmem((share, 128), BF16),
            vmem((128, 128), F32),
            vmem((2, 8, 128), F32),
            vmem((2, 4, 8, 128), F32),
            vmem((2, 8, 128), F32),
            vmem((2, nz, 8, 128), F32),
            vmem((8, 128), F32),
            vmem((nb, 8, 128), F32),
            pltpu.SemaphoreType.DMA((9,)),
            pltpu.SemaphoreType.DMA((copies,)),
            pltpu.SemaphoreType.DMA((copies,)),
        ],
        compiler_params=pltpu.CompilerParams(
            collective_id=0, has_side_effects=True, vmem_limit_bytes=60 * 1024 * 1024
        ),
    )(
        inputs, out_grads, kernel.transpose(0, 1, 3, 2, 4),
        norm_gain.reshape(1, CH), norm_shift.reshape(1, CH),
    )
    out, grad, gain, shift = pl.pallas_call(
        unpack_body,
        out_shape=(
            jax.ShapeDtypeStruct((FRAMES, ROWS, CH, COLS), BF16),
            jax.ShapeDtypeStruct((3, 3, 3, CH, CH), F32),
            jax.ShapeDtypeStruct((1, CH), F32),
            jax.ShapeDtypeStruct((1, CH), F32),
        ),
        in_specs=[any_space] * 3,
        out_specs=(any_space,) * 4,
        scratch_shapes=[
            vmem((FRAMES, ROWS, CH, COLS), BF16),
            vmem((FLAT, 128), BF16),
            vmem((8, 128), F32),
            vmem((2, 8, CH), F32),
            vmem((3, 3, 3, CH, CH), F32),
            pltpu.SemaphoreType.DMA((11,)),
        ],
        compiler_params=pltpu.CompilerParams(vmem_limit_bytes=60 * 1024 * 1024),
    )(out, final, small)
    return (out, grad.transpose(0, 1, 3, 2, 4), gain.reshape(CH), shift.reshape(CH))


def solution(mesh):
    sizes = (mesh.shape["block"], mesh.shape["tile"] // 4)
    placed = (P("block", "tile", None, None), P("block", "tile", None, None), P(), P(), P())
    return jax.shard_map(
        functools.partial(shards, sizes),
        mesh=mesh,
        in_specs=placed,
        out_specs=(P("block", "tile", None, None), P(), P(), P()),
        check_vma=False,
    )
```
